32 devices in a mesh: lon: 8 (over y, x, core), lat: 4 (over z).
Axes of the slice: x: 2, y: 2, z: 4, core: 2. Of those that a mesh axis runs over, the one named last changes fastest.
Arguments:
- tokens: bfloat16 [96, 32, 1024], P('lon', 'lat'), may hold values from -6 to 6
- query_local: bfloat16 [96, 32, 1024], P('lon', 'lat'), may hold values from -21 to 21, as said below
- key_local: bfloat16 [96, 32, 1024], P('lon', 'lat'), may hold values from -21 to 21, as said below
- value_local: bfloat16 [96, 32, 1024], P('lon', 'lat'), may hold values from -6 to 6
- position_bias: float32 [16, 13, 13], replicated, may hold values from -4 to 4
- output_weight: bfloat16 [1024, 1024], P('lat'), may hold values from -0.1875 to 0.1875
- norm_gain: float32 [1024], replicated, may hold values from 0.1 to 1.9
- global_weight: bfloat16 [1024, 3072], P('lat'), may hold values from -1 to 1
Outputs:
- hidden: bfloat16 [96, 32, 1024], P('lon', 'lat')
- attended: bfloat16 [96, 32, 1024], P('lon', 'lat')
The draws below stay inside these ranges and needn't reach their ends.
Inputs may be any that keep to these rules, and one draw needn't show every extreme that they name: `query_local`: entries of the neighbourhood queries and keys. `key_local`: entries of the neighbourhood queries and keys.
All inputs are finite; a program needn't handle non-finite values.
Results may differ from the reference program's by a relative error of at most 0.015.
Values may be sent and summed in bfloat16 or wider, within the bound.
A program may use at most 64 MiB of HBM per device.

```python
import math
import jax
import jax.numpy as jnp
from jax import lax

D = 1024
HEADS = 16
TLON = 12
TLAT = 8
RADIUS = 6
WINDOW = 13
STEPS = 4
NLON = 96
NLAT = 32
N_LON = 8
N_LAT = 4


def make_pair(key):
    shape = (NLON, NLAT, D)
    query_key = jax.random.fold_in(key, 11)
    keys_key = jax.random.fold_in(key, 12)
    query = jnp.clip(jax.random.normal(query_key, shape, jnp.float32), -6.0, 6.0)
    keys = jnp.clip(jax.random.normal(keys_key, shape, jnp.float32), -6.0, 6.0)
    return (query, keys)


def draw_query_local(key, part):
    return make_pair(key)[0].astype(jnp.bfloat16)


def draw_key_local(key, part):
    return make_pair(key)[1].astype(jnp.bfloat16)


def draw_tokens(key, part):
    shape = (NLON, NLAT, D)
    values = jax.random.normal(jax.random.fold_in(key, 34), shape, jnp.float32)
    return jnp.clip(values, -6.0, 6.0).astype(jnp.bfloat16)


def draw_global_weight(key, part):
    shape = (D, 3 * D)
    spread = 1.0 / D ** 0.5
    values = jnp.clip(jax.random.normal(jax.random.fold_in(key, 42), shape, jnp.float32), -6.0, 6.0) * spread
    return jnp.clip(values, -1.0, 1.0).astype(jnp.bfloat16)


def level_of(stream_key, extent, split, least, high):
    level, own = 1.0, jax.random.fold_in(stream_key, 6)
    for axis_at, parts in split:
        heights = jnp.exp(jax.random.uniform(jax.random.fold_in(own, axis_at), (parts,), jnp.float32, least / len(split), high / len(split)))
        level = level * jnp.repeat(heights, extent[axis_at] // parts).reshape([-1 if axis == axis_at else 1 for axis in range(len(extent))])
    return level


def centred(key, shape, scale, most, shards=(), held_as=jnp.bfloat16):
    values = scale * jax.random.normal(key, shape, jnp.float32)
    if shards:
        values = values * level_of(key, shape, shards, -0.22, 0.18)
    return jnp.clip(values, -most, most).astype(held_as)


def setup_inputs(seed: int = 0) -> dict:
    splits = jax.random.split(jax.random.key(seed), 9)
    return {
        "tokens": draw_tokens(jax.random.fold_in(splits[8], 71), 0),
        "query_local": draw_query_local(jax.random.fold_in(splits[8], 71), 0),
        "key_local": draw_key_local(jax.random.fold_in(splits[8], 71), 0),
        "value_local": centred(splits[3], (NLON, NLAT, D), 1.0, 6.0, ((0, 8), (1, 4))),
        "position_bias": centred(splits[4], (HEADS, WINDOW, WINDOW), 1.0, 4.0, (), jnp.float32),
        "output_weight": centred(splits[5], (D, D), D ** -0.5, 0.1875, ((0, 4),)),
        "norm_gain": jnp.clip(1.0 + 0.18 * jax.random.normal(splits[6], (D,), jnp.float32), 0.1, 1.9),
        "global_weight": draw_global_weight(jax.random.fold_in(splits[8], 71), 0),
    }


def neighbour_layer(query_local, key_local, value_local, position_bias):
    head_size = D // HEADS
    score_scale = 1.0 / math.sqrt(head_size)
    padded_key = jnp.pad(key_local, ((0, 0), (RADIUS, RADIUS), (0, 0)))
    padded_value = jnp.pad(value_local, ((0, 0), (RADIUS, RADIUS), (0, 0)))
    lat_index = jnp.arange(NLAT + 2 * RADIUS, dtype=jnp.int32) - RADIUS
    lat_inside = (lat_index >= 0) & (lat_index < NLAT)

    def one_block(row_start):
        source_rows = (row_start + jnp.arange(TLON + 2 * RADIUS, dtype=jnp.int32) - RADIUS) % NLON
        key_slab = jnp.take(padded_key, source_rows, axis=0).astype(jnp.float32)
        value_slab = jnp.take(padded_value, source_rows, axis=0).astype(jnp.float32)
        query_block = lax.dynamic_slice_in_dim(query_local, row_start, TLON, 0).astype(jnp.float32)
        query_block = query_block.reshape(TLON, NLAT, HEADS, head_size)
        score_list = []
        for lon_offset in range(WINDOW):
            for lat_offset in range(WINDOW):
                key_part = key_slab[lon_offset:lon_offset + TLON, lat_offset:lat_offset + NLAT]
                key_part = key_part.reshape(TLON, NLAT, HEADS, head_size)
                score_one = jnp.einsum('abhd,abhd->abh', query_block, key_part) * score_scale
                score_one = score_one + position_bias[:, lon_offset, lat_offset]
                valid_one = lat_inside[lat_offset:lat_offset + NLAT][None, :, None]
                score_list.append(jnp.where(valid_one, score_one, -1e+30))
        scores = jnp.stack(score_list, axis=-1)
        largest = lax.optimization_barrier(jnp.max(scores, axis=-1, keepdims=True))
        weights = jnp.exp(scores - largest)
        denominator = lax.optimization_barrier(jnp.sum(weights, axis=-1))
        rounded = lax.optimization_barrier(weights.astype(jnp.bfloat16)).astype(jnp.float32)
        accumulated = jnp.zeros((TLON, NLAT, HEADS, head_size), jnp.float32)
        position = 0
        for lon_offset in range(WINDOW):
            for lat_offset in range(WINDOW):
                value_part = value_slab[lon_offset:lon_offset + TLON, lat_offset:lat_offset + NLAT]
                value_part = value_part.reshape(TLON, NLAT, HEADS, head_size)
                accumulated = accumulated + rounded[..., position][..., None] * value_part
                position = position + 1
        result = accumulated / denominator[..., None]
        return result.reshape(TLON, NLAT, D).astype(jnp.bfloat16)
    starts = jnp.arange(N_LON, dtype=jnp.int32) * TLON
    blocks_out = lax.map(one_block, starts)
    return blocks_out.reshape(NLON, NLAT, D)

def to_blocks(array):
    channels = array.shape[-1]
    shaped = array.reshape(N_LON, TLON, N_LAT, TLAT, channels).transpose(0, 2, 1, 3, 4)
    return shaped.reshape(N_LON * N_LAT, TLON * TLAT, channels)

def from_blocks(array):
    channels = array.shape[-1]
    shaped = array.reshape(N_LON, N_LAT, TLON, TLAT, channels).transpose(0, 2, 1, 3, 4)
    return shaped.reshape(NLON, NLAT, channels)

def reference(tokens, query_local, key_local, value_local, position_bias, output_weight, norm_gain, global_weight):
    head_size = D // HEADS
    score_scale = 1.0 / math.sqrt(head_size)
    local_out = neighbour_layer(query_local, key_local, value_local, position_bias)
    flat_local = local_out.reshape(NLON * NLAT, D)
    projected = jnp.dot(flat_local, output_weight, preferred_element_type=jnp.float32)
    hidden = (tokens.reshape(NLON * NLAT, D).astype(jnp.float32) + projected).astype(jnp.bfloat16)
    widened = hidden.astype(jnp.float32)
    inverse = lax.rsqrt(lax.optimization_barrier(jnp.mean(widened * widened, axis=1, keepdims=True)) + 1e-06)
    normed = (widened * inverse * norm_gain.astype(jnp.float32)).astype(jnp.bfloat16)
    triple = jnp.dot(normed, global_weight, preferred_element_type=jnp.float32).astype(jnp.bfloat16)
    grid_triple = triple.reshape(NLON, NLAT, 3 * D)
    query_blocks = to_blocks(grid_triple[:, :, :D])
    key_blocks = to_blocks(grid_triple[:, :, D:2 * D])
    value_blocks = to_blocks(grid_triple[:, :, 2 * D:])
    block_count = N_LON * N_LAT

    def attend_block(block_index):
        sources = (block_index - jnp.arange(STEPS + 1, dtype=jnp.int32)) % block_count
        keys_near = jnp.take(key_blocks, sources, axis=0).reshape(-1, HEADS, head_size).astype(jnp.float32)
        values_near = jnp.take(value_blocks, sources, axis=0).reshape(-1, HEADS, head_size).astype(jnp.float32)
        query_here = lax.dynamic_index_in_dim(query_blocks, block_index, 0, keepdims=False)
        query_here = query_here.reshape(-1, HEADS, head_size).astype(jnp.float32)
        scores = jnp.einsum('qhd,khd->hqk', query_here, keys_near) * score_scale
        largest = lax.optimization_barrier(jnp.max(scores, axis=2, keepdims=True))
        weights = jnp.exp(scores - largest)
        denominator = lax.optimization_barrier(jnp.sum(weights, axis=2))
        rounded = lax.optimization_barrier(weights.astype(jnp.bfloat16)).astype(jnp.float32)
        weighted = jnp.einsum('hqk,khd->qhd', rounded, values_near)
        result = weighted / jnp.transpose(denominator)[:, :, None]
        return result.reshape(-1, D).astype(jnp.bfloat16)
    attended_blocks = lax.map(attend_block, jnp.arange(block_count, dtype=jnp.int32))
    attended = from_blocks(attended_blocks)
    return (hidden.reshape(NLON, NLAT, D), attended)
```

```python
import functools

import jax
import jax.numpy as jnp
from jax import lax
from jax.experimental import pallas as pl
from jax.experimental.pallas import tpu as pltpu
from jax.sharding import PartitionSpec as P

STEPS = 4
CHUNKS = 4
NEG = -1e30
MESH = pl.DeviceIdType.MESH


def kernel(
    n_lon,
    n_lat,
    pieces,
    tok_ref,
    q_ref,
    k_hbm,
    v_hbm,
    b_ref,
    wo_hbm,
    gain_ref,
    wg_hbm,
    hid_ref,
    att_ref,
    kbuf,
    vbuf,
    wo,
    wg,
    rbuf,
    lo,
    nbuf,
    gq,
    gk,
    gv,
    own_sem,
    lat_s,
    lat_r,
    lon_s,
    lon_r,
    w1_s,
    w1_r,
    wp_s,
    wp_r,
    wa_s,
    wa_r,
    wb_s,
    wb_r,
    ex_s,
    ex_r,
):
    i = lax.axis_index("lon")
    z = lax.axis_index("lat")
    rows = wo_hbm.shape[0]
    part = rows // pieces
    tokens, width = tok_ref.shape
    half = tokens // 2
    seg = 2 * tokens
    cw = width // CHUNKS
    j = lax.rem(i, pieces)
    base = i - j
    mate = base + j + 1 - 2 * lax.rem(j, 2)
    hops = pieces // 2 - 1
    p = i * n_lat + z
    total = n_lon * n_lat

    def lat_dev(d):
        return (i, lax.rem(z + d + n_lat, n_lat))

    def lon_dev(d):
        return (lax.rem(i + d + n_lon, n_lon), z)

    def peer(k):
        return base + lax.rem(j + 2 * k + pieces, pieces)

    def line_dev(s):
        t = lax.rem(p + s + total, total)
        return (t // n_lat, lax.rem(t, n_lat))

    def rc(src, dst, ssem, rsem, dev):
        return pltpu.make_async_remote_copy(
            src_ref=src, dst_ref=dst, send_sem=ssem, recv_sem=rsem, device_id=dev, device_id_type=MESH
        )

    barrier = pltpu.get_barrier_semaphore()
    greet = [lat_dev(-d) for d in range(1, n_lat)]
    greet += [lon_dev(1), lon_dev(-1), (mate, z)]
    greet += [(peer(-k), z) for k in range(1, hops + 1)]
    greet += [line_dev(-s) for s in range(1, STEPS + 1)]
    for dev in greet:
        pl.semaphore_signal(barrier, inc=1, device_id=dev, device_id_type=MESH)

    pairs = ((k_hbm, kbuf), (v_hbm, vbuf))
    weights = ((wo_hbm, wo), (wg_hbm, wg))
    own_copies = []
    for a, (src, dst) in enumerate(pairs):
        own_copies.append(
            pltpu.make_async_copy(src, dst.at[pl.ds(seg + half, tokens)], own_sem.at[a])
        )
    for a, (src, dst) in enumerate(weights):
        own_copies.append(
            pltpu.make_async_copy(
                src, dst.at[pl.ds(pl.multiple_of(z * rows, 16), rows)], own_sem.at[2 + a]
            )
        )
    for copy in own_copies:
        copy.start()
    pl.semaphore_wait(barrier, len(greet))

    def cols(c):
        return pl.ds(c * cw, cw)

    def lat_copy(a, way, c):
        src, dst = pairs[a]
        at = 0 if way == 0 else 2
        return rc(
            src.at[:, cols(c)],
            dst.at[pl.ds(at * seg + half, tokens), cols(c)],
            lat_s.at[a, way, c],
            lat_r.at[a, way, c],
            lat_dev(1 if way == 0 else -1),
        )

    def lon_copy(a, s, way, c):
        src, dst = pairs[a]
        if s == 1:
            source = src.at[pl.ds(half if way == 0 else 0, half), cols(c)]
        else:
            source = dst.at[pl.ds(s * seg + (tokens if way == 0 else half), half), cols(c)]
        return rc(
            source,
            dst.at[pl.ds(s * seg + (0 if way == 0 else half + tokens), half), cols(c)],
            lon_s.at[a, s, way, c],
            lon_r.at[a, s, way, c],
            lon_dev(1 if way == 0 else -1),
        )

    has_up = z < n_lat - 1
    has_down = z > 0

    for c in range(CHUNKS):
        @pl.when(has_up)
        def _():
            for a in range(2):
                lat_copy(a, 0, c).start()

        @pl.when(has_down)
        def _():
            for a in range(2):
                lat_copy(a, 1, c).start()

        for a in range(2):
            for way in range(2):
                lon_copy(a, 1, way, c).start()

    def w_rows(shard, piece):
        return pl.ds(pl.multiple_of(shard * rows + piece * part, 16), part)

    def w1_copy(a, d):
        src, dst = weights[a]
        return rc(
            src.at[pl.ds(pl.multiple_of(j * part, 16), part)],
            dst.at[w_rows(z, j)],
            w1_s.at[a, d],
            w1_r.at[a, d],
            lat_dev(d),
        )

    def w_move(a, d, piece, ssem, rsem, dev):
        ref = weights[a][1].at[w_rows(lax.rem(z - d + n_lat, n_lat), piece)]
        return rc(ref, ref, ssem, rsem, dev)

    def w1_wait(a, d):
        w_move(a, d, j, w1_s.at[a, d], w1_r.at[a, d], lat_dev(d)).wait_recv()

    def wp_copy(a, d, piece):
        return w_move(a, d, piece, wp_s.at[a, d], wp_r.at[a, d], (mate, z))

    def wa_copy(a, d, k, piece):
        return w_move(a, d, piece, wa_s.at[a, d, k], wa_r.at[a, d, k], (peer(k), z))

    def wb_copy(a, d, k, piece):
        return w_move(a, d, piece, wb_s.at[a, d, k], wb_r.at[a, d, k], (mate, z))

    mate_piece = mate - base

    def far_piece(k):
        return lax.rem(j - 2 * k + pieces, pieces)

    def mate_far_piece(k):
        return lax.rem(mate_piece - 2 * k + pieces, pieces)

    def spread(a):
        for d in range(1, n_lat):
            w1_wait(a, d)
            wp_copy(a, d, j).start()
            for k in range(1, hops + 1):
                wa_copy(a, d, k, j).start()

    def relay(a):
        for d in range(1, n_lat):
            for k in range(1, hops + 1):
                wa_copy(a, d, k, far_piece(k)).wait_recv()
                wb_copy(a, d, k, far_piece(k)).start()

    def gathered(a):
        own_copies[2 + a].wait()
        for d in range(1, n_lat):
            wp_copy(a, d, mate_piece).wait_recv()
            for k in range(1, hops + 1):
                wb_copy(a, d, k, mate_far_piece(k)).wait_recv()

    for a in range(2):
        for d in range(1, n_lat):
            w1_copy(a, d).start()

    pad_rows = kbuf.shape[0] - 3 * seg
    for ref in (kbuf, vbuf):
        ref[pl.ds(3 * seg, pad_rows), :] = jnp.zeros((pad_rows, width), jnp.bfloat16)

        @pl.when(jnp.logical_not(has_down))
        def _():
            ref[pl.ds(0, seg), :] = jnp.zeros((seg, width), jnp.bfloat16)

        @pl.when(jnp.logical_not(has_up))
        def _():
            ref[pl.ds(2 * seg, seg), :] = jnp.zeros((seg, width), jnp.bfloat16)

    for ref in (gk, gv):
        pad = ref.shape[0] - (STEPS + 1) * tokens
        ref[pl.ds((STEPS + 1) * tokens, pad), :] = jnp.zeros((pad, width), jnp.bfloat16)

    lanes = kbuf.shape[0]
    flat = b_ref[...]
    row_id = lax.broadcasted_iota(jnp.int32, flat.shape, 0)
    shifted = jnp.zeros_like(flat)
    for r in range(8):
        shifted = jnp.where(lax.rem(row_id, 8) == r, pltpu.roll(flat, r + 2, 1), shifted)
    lane = lax.broadcasted_iota(jnp.int32, (flat.shape[1], lanes), 1)
    spot = lax.broadcasted_iota(jnp.int32, (flat.shape[1], lanes), 0)
    at_seg = (lane >= seg).astype(jnp.int32) + (lane >= 2 * seg).astype(jnp.int32)
    inner = lane - at_seg * seg
    wanted = lax.shift_right_logical(inner, 3) * 24 + at_seg * 8 + (inner & 7)
    pick = jnp.where(spot == wanted, 1.0, 0.0).astype(jnp.bfloat16)
    first = shifted.astype(jnp.bfloat16)
    rest = shifted - first.astype(jnp.float32)
    second = rest.astype(jnp.bfloat16)
    third = (rest - second.astype(jnp.float32)).astype(jnp.bfloat16)
    bias = jnp.dot(first, pick, preferred_element_type=jnp.float32)
    bias = bias + jnp.dot(second, pick, preferred_element_type=jnp.float32)
    bias = bias + jnp.dot(third, pick, preferred_element_type=jnp.float32)
    lane = lax.broadcasted_iota(jnp.int32, bias.shape, 1)
    jrow = lax.rem(lax.broadcasted_iota(jnp.int32, bias.shape, 0), 8)
    at_seg = (lane >= seg).astype(jnp.int32) + (lane >= 2 * seg).astype(jnp.int32)
    inner = lane - at_seg * seg
    index = at_seg * 8 + (inner & 7) - jrow - 2
    low_lane = jnp.where(has_down, 0, seg)
    high_lane = jnp.where(has_up, 3 * seg, 2 * seg)
    fits = (inner < 13 * 8) & (index >= 0) & (index < 13) & (lane >= low_lane) & (lane < high_lane)
    rbuf[...] = jnp.where(fits, bias, NEG)

    def forward(c):
        @pl.when(has_down)
        def _():
            for a in range(2):
                lat_copy(a, 0, c).wait_recv()
                for way in range(2):
                    lon_copy(a, 0, way, c).start()

        @pl.when(has_up)
        def _():
            for a in range(2):
                lat_copy(a, 1, c).wait_recv()
                for way in range(2):
                    lon_copy(a, 2, way, c).start()

    def landed(c):
        for a in range(2):
            for way in range(2):
                lon_copy(a, 1, way, c).wait_recv()

        @pl.when(has_down)
        def _():
            for a in range(2):
                for way in range(2):
                    lon_copy(a, 0, way, c).wait_recv()

        @pl.when(has_up)
        def _():
            for a in range(2):
                for way in range(2):
                    lon_copy(a, 2, way, c).wait_recv()

    left = (lax.broadcasted_iota(jnp.int32, (tokens, 128), 1) < 64).astype(jnp.float32)
    left_mask = left.astype(jnp.bfloat16)
    right_mask = (1.0 - left).astype(jnp.bfloat16)

    def two_heads(q2, k2, v2, fix):
        qq = jnp.concatenate([q2 * left_mask, q2 * right_mask], axis=0)
        s = lax.dot_general(qq, k2, (((1,), (1,)), ((), ())), preferred_element_type=jnp.float32)
        s = fix(s * 0.125)
        e = jnp.exp(s - jnp.max(s, axis=1, keepdims=True))
        t = jnp.sum(e, axis=1, keepdims=True)
        o = jnp.dot(e.astype(jnp.bfloat16), v2, preferred_element_type=jnp.float32) / t
        return jnp.where(left > 0.5, o[:tokens], o[tokens:]).astype(jnp.bfloat16)

    def local_pair(h):
        at = pl.ds(pl.multiple_of(h * 128, 128), 128)

        def fix(s):
            parts = []
            for head in range(2):
                r = rbuf[pl.ds(pl.multiple_of(h * 16 + head * 8, 8), 8), :]
                for col in range(tokens // 8):
                    parts.append(r if col == 0 else pltpu.roll(r, col * 8, 1))
            return s + jnp.concatenate(parts, axis=0)

        lo[:, at] = two_heads(q_ref[:, at], kbuf[:, at], vbuf[:, at], fix)

    per = cw // 128
    for c in range(CHUNKS):
        forward(c)
    spread(0)
    for copy in own_copies[:2]:
        copy.wait()
    for c in range(CHUNKS):
        landed(c)
        pl.loop(c * per, (c + 1) * per)(local_pair)
        if c == 0:
            spread(1)
        if c == CHUNKS - 2:
            relay(0)
    gathered(0)

    projected = jnp.dot(lo[...], wo[...], preferred_element_type=jnp.float32)
    hidden = (tok_ref[...].astype(jnp.float32) + projected).astype(jnp.bfloat16)
    hid_ref[...] = hidden
    wide = hidden.astype(jnp.float32)
    inverse = lax.rsqrt(jnp.mean(wide * wide, axis=1, keepdims=True) + 1e-06)
    nbuf[pl.ds(0, tokens), :] = (wide * inverse * gain_ref[...]).astype(jnp.bfloat16)

    def ex_copy(s):
        return rc(
            nbuf.at[pl.ds(0, tokens)],
            nbuf.at[pl.ds(s * tokens, tokens)],
            ex_s.at[s],
            ex_r.at[s],
            line_dev(s),
        )

    for s in range(1, STEPS + 1):
        ex_copy(s).start()
    relay(1)
    gathered(1)

    tile = 512

    def project(at, count, column):
        left_rows = nbuf[pl.ds(at, count), :]
        weight = wg[:, pl.ds(pl.multiple_of(column, tile), tile)]
        return jnp.dot(left_rows, weight, preferred_element_type=jnp.float32).astype(jnp.bfloat16)

    def keys_values(at, count):
        @pl.loop(0, width // tile)
        def _(t):
            here = pl.ds(pl.multiple_of(t * tile, tile), tile)
            gk[pl.ds(at, count), here] = project(at, count, width + t * tile)
            gv[pl.ds(at, count), here] = project(at, count, 2 * width + t * tile)

    @pl.loop(0, width // tile)
    def _(t):
        here = pl.ds(pl.multiple_of(t * tile, tile), tile)
        gq[:, here] = project(0, tokens, t * tile)

    keys_values(0, tokens)
    for s in range(1, STEPS + 1):
        ex_copy(s).wait_recv()
        if s % 2 == 0:
            keys_values((s - 1) * tokens, 2 * tokens)

    def global_pair(h):
        at = pl.ds(pl.multiple_of(h * 128, 128), 128)

        def fix(s):
            key = lax.broadcasted_iota(jnp.int32, s.shape, 1)
            return jnp.where(key < (STEPS + 1) * tokens, s, NEG)

        att_ref[:, at] = two_heads(gq[:, at], gk[:, at], gv[:, at], fix)

    pl.loop(0, width // 128)(global_pair)

    for c in range(CHUNKS):
        for a in range(2):
            for way in range(2):
                lon_copy(a, 1, way, c).wait_send()

        @pl.when(has_up)
        def _():
            for a in range(2):
                lat_copy(a, 0, c).wait_send()
                for way in range(2):
                    lon_copy(a, 2, way, c).wait_send()

        @pl.when(has_down)
        def _():
            for a in range(2):
                lat_copy(a, 1, c).wait_send()
                for way in range(2):
                    lon_copy(a, 0, way, c).wait_send()

    for a in range(2):
        for d in range(1, n_lat):
            w1_copy(a, d).wait_send()
            wp_copy(a, d, j).wait_send()
            for k in range(1, hops + 1):
                wa_copy(a, d, k, j).wait_send()
                wb_copy(a, d, k, far_piece(k)).wait_send()
    for s in range(1, STEPS + 1):
        ex_copy(s).wait_send()


def body(tokens, query_local, key_local, value_local, position_bias, output_weight, norm_gain, global_weight):
    n_lon = lax.axis_size("lon")
    n_lat = lax.axis_size("lat")
    lon_cells, lat_cells, width = tokens.shape
    count = lon_cells * lat_cells
    heads, window, _ = position_bias.shape
    rows = output_weight.shape[0]
    pieces = min(n_lon, rows // 16)
    hops = pieces // 2

    def flat(x):
        return x.reshape(count, width)

    table = jnp.pad(position_bias, ((0, 0), (0, 0), (0, 24 - window))).reshape(heads, window * 24)
    table = jnp.pad(table, ((0, 0), (0, 384 - window * 24)))
    table = jnp.broadcast_to(table[:, None, :], (heads, 8, 384)).reshape(heads * 8, 384)
    lanes = -(-(6 * count) // 128) * 128
    keys = -(-((STEPS + 1) * count) // 128) * 128
    vmem = pl.BlockSpec(memory_space=pltpu.VMEM)
    hbm = pl.BlockSpec(memory_space=pl.ANY)
    dma = pltpu.SemaphoreType.DMA
    bf16 = jnp.bfloat16
    hidden, attended = pl.pallas_call(
        functools.partial(kernel, n_lon, n_lat, pieces),
        out_shape=(jax.ShapeDtypeStruct((count, width), bf16),) * 2,
        in_specs=[vmem, vmem, hbm, hbm, vmem, hbm, vmem, hbm],
        out_specs=(vmem, vmem),
        scratch_shapes=[
            pltpu.VMEM((lanes, width), bf16),
            pltpu.VMEM((lanes, width), bf16),
            pltpu.VMEM((width, width), bf16),
            pltpu.VMEM((width, 3 * width), bf16),
            pltpu.VMEM((heads * 8, lanes), jnp.float32),
            pltpu.VMEM((count, width), bf16),
            pltpu.VMEM(((STEPS + 1) * count, width), bf16),
            pltpu.VMEM((count, width), bf16),
            pltpu.VMEM((keys, width), bf16),
            pltpu.VMEM((keys, width), bf16),
            dma((4,)),
            dma((2, 2, CHUNKS)),
            dma((2, 2, CHUNKS)),
            dma((2, 3, 2, CHUNKS)),
            dma((2, 3, 2, CHUNKS)),
            dma((2, n_lat)),
            dma((2, n_lat)),
            dma((2, n_lat)),
            dma((2, n_lat)),
            dma((2, n_lat, hops)),
            dma((2, n_lat, hops)),
            dma((2, n_lat, hops)),
            dma((2, n_lat, hops)),
            dma((STEPS + 1,)),
            dma((STEPS + 1,)),
        ],
        compiler_params=pltpu.CompilerParams(
            collective_id=0, has_side_effects=True, vmem_limit_bytes=48 * 1024 * 1024
        ),
    )(
        flat(tokens),
        flat(query_local),
        flat(key_local),
        flat(value_local),
        table,
        output_weight,
        norm_gain.reshape(1, width),
        global_weight,
    )
    return hidden.reshape(tokens.shape), attended.reshape(tokens.shape)


def solution(mesh):
    return jax.shard_map(
        body,
        mesh=mesh,
        in_specs=(
            P("lon", "lat", None),
            P("lon", "lat", None),
            P("lon", "lat", None),
            P("lon", "lat", None),
            P(),
            P("lat", None),
            P(),
            P("lat", None),
        ),
        out_specs=(P("lon", "lat", None), P("lon", "lat", None)),
        check_vma=False,
    )
```

```python
import functools

import jax
import jax.numpy as jnp
from jax import lax
from jax.experimental import pallas as pl
from jax.experimental.pallas import tpu as pltpu
from jax.sharding import PartitionSpec as P

STEPS = 4
CHUNKS = 4
NEG = -1e30
MESH = pl.DeviceIdType.MESH


def kernel(
    n_lon,
    n_lat,
    pieces,
    tok_hbm,
    q_hbm,
    k_hbm,
    v_hbm,
    b_hbm,
    wo_hbm,
    gain_hbm,
    wg_hbm,
    hid_ref,
    att_ref,
    tok_ref,
    q_ref,
    b_ref,
    gain_ref,
    kbuf,
    vbuf,
    wo,
    wg,
    rbuf,
    lo,
    nbuf,
    gq,
    gk,
    gv,
    own_sem,
    lat_s,
    lat_r,
    lon_s,
    lon_r,
    w1_s,
    w1_r,
    wp_s,
    wp_r,
    wx_s,
    wx_r,
    wh_s,
    wh_r,
    wm_s,
    wm_r,
    ex_s,
    ex_r,
):
    i = lax.axis_index("lon")
    z = lax.axis_index("lat")
    rows = wo_hbm.shape[0]
    part = rows // pieces
    tokens, width = tok_ref.shape
    half = tokens // 2
    seg = 2 * tokens
    cw = width // CHUNKS
    j = lax.rem(i, pieces)
    base = i - j
    dims = pieces.bit_length() - 2

    def flip(at, bit):
        return at + bit - 2 * bit * lax.rem(at // bit, 2)

    mate = base + flip(j, 1)
    p = i * n_lat + z
    total = n_lon * n_lat

    def lat_dev(d):
        return (i, lax.rem(z + d + n_lat, n_lat))

    def lon_dev(d):
        return (lax.rem(i + d + n_lon, n_lon), z)

    def side(e):
        return (base + flip(j, 2 << e), z)

    def line_dev(s):
        t = lax.rem(p + s + total, total)
        return (t // n_lat, lax.rem(t, n_lat))

    def rc(src, dst, ssem, rsem, dev):
        return pltpu.make_async_remote_copy(
            src_ref=src, dst_ref=dst, send_sem=ssem, recv_sem=rsem, device_id=dev, device_id_type=MESH
        )

    barrier = pltpu.get_barrier_semaphore()
    greet = [lat_dev(-d) for d in range(1, n_lat)]
    greet += [lon_dev(1), lon_dev(-1), (mate, z)]
    greet += [side(e) for e in range(dims)]
    greet += [line_dev(-s) for s in range(1, STEPS + 1)]
    for dev in greet:
        pl.semaphore_signal(barrier, inc=1, device_id=dev, device_id_type=MESH)

    pairs = ((k_hbm, kbuf), (v_hbm, vbuf))
    weights = ((wo_hbm, wo), (wg_hbm, wg))
    own_copies = []
    for a, (src, dst) in enumerate(pairs):
        own_copies.append(
            pltpu.make_async_copy(src, dst.at[pl.ds(seg + half, tokens)], own_sem.at[a])
        )
    for a, (src, dst) in enumerate(weights):
        own_copies.append(
            pltpu.make_async_copy(
                src, dst.at[pl.ds(pl.multiple_of(z * rows, 16), rows)], own_sem.at[2 + a]
            )
        )
    singles = ((b_hbm, b_ref), (q_hbm, q_ref), (tok_hbm, tok_ref), (gain_hbm, gain_ref))
    for a, (src, dst) in enumerate(singles):
        own_copies.append(pltpu.make_async_copy(src, dst, own_sem.at[4 + a]))
    for at in (4, 0, 1, 5, 2, 3, 6, 7):
        own_copies[at].start()
    pl.semaphore_wait(barrier, len(greet))

    def cols(c):
        return pl.ds(c * cw, cw)

    def lat_copy(a, way, c):
        src, dst = pairs[a]
        at = 0 if way == 0 else 2
        return rc(
            src.at[:, cols(c)],
            dst.at[pl.ds(at * seg + half, tokens), cols(c)],
            lat_s.at[a, way, c],
            lat_r.at[a, way, c],
            lat_dev(1 if way == 0 else -1),
        )

    def lon_copy(a, s, way, c):
        src, dst = pairs[a]
        if s == 1:
            source = src.at[pl.ds(half if way == 0 else 0, half), cols(c)]
        else:
            source = dst.at[pl.ds(s * seg + (tokens if way == 0 else half), half), cols(c)]
        return rc(
            source,
            dst.at[pl.ds(s * seg + (0 if way == 0 else half + tokens), half), cols(c)],
            lon_s.at[a, s, way, c],
            lon_r.at[a, s, way, c],
            lon_dev(1 if way == 0 else -1),
        )

    has_up = z < n_lat - 1
    has_down = z > 0

    def w_rows(shard, piece):
        return pl.ds(pl.multiple_of(shard * rows + piece * part, 16), part)

    def w1_copy(a, d):
        src, dst = weights[a]
        return rc(
            src.at[pl.ds(pl.multiple_of(j * part, 16), part)],
            dst.at[w_rows(z, j)],
            w1_s.at[a, d],
            w1_r.at[a, d],
            lat_dev(d),
        )

    def w_move(a, d, piece, ssem, rsem, dev):
        ref = weights[a][1].at[w_rows(lax.rem(z - d + n_lat, n_lat), piece)]
        return rc(ref, ref, ssem, rsem, dev)

    def w1_wait(a, d):
        w_move(a, d, j, w1_s.at[a, d], w1_r.at[a, d], lat_dev(d)).wait_recv()

    def wp_copy(a, d, piece):
        return w_move(a, d, piece, wp_s.at[a, d], wp_r.at[a, d], (mate, z))

    def w_half(a, d, piece, e, ssem, rsem, dev):
        size = part // 2
        at = lax.rem(z - d + n_lat, n_lat) * rows + piece * part + e * size
        ref = weights[a][1].at[pl.ds(pl.multiple_of(at, 16), size)]
        return rc(ref, ref, ssem, rsem, dev)

    def wx_copy(a, d, e, piece):
        return w_move(a, d, piece, wx_s.at[a, d, e], wx_r.at[a, d, e], side(e))

    def wh_copy(a, d, e, piece):
        return w_half(a, d, piece, e, wh_s.at[a, d, e], wh_r.at[a, d, e], side(1 - e))

    def wm_copy(a, d, e, piece):
        return w_move(a, d, piece, wm_s.at[a, d, e], wm_r.at[a, d, e], (mate, z))

    mate_piece = flip(j, 1)
    corners = 1 if dims == 2 else 0

    def across(at, e):
        return flip(at, 2 << e) if e < 2 else flip(flip(at, 2), 4)

    def spread(a, ds):
        for d in ds:
            w1_wait(a, d)
            for e in range(dims):
                wx_copy(a, d, e, j).start()
            wp_copy(a, d, j).start()

    def relay(a, ds):
        for d in ds:
            for e in range(dims):
                piece = across(j, e)
                wx_copy(a, d, e, piece).wait_recv()
                if corners:
                    wh_copy(a, d, e, piece).start()
                wm_copy(a, d, e, piece).start()

    def corner(a, ds):
        if corners:
            for d in ds:
                piece = across(j, 2)
                for e in range(2):
                    wh_copy(a, d, e, piece).wait_recv()
                wm_copy(a, d, 2, piece).start()

    def gathered(a):
        own_copies[2 + a].wait()
        for d in near:
            wp_copy(a, d, mate_piece).wait_recv()
            for e in range(dims + corners):
                wm_copy(a, d, e, across(mate_piece, e)).wait_recv()

    near = sorted(range(1, n_lat), key=lambda d: min(d, n_lat - d))
    third = len(near) // 3
    thirds = (near[:third], near[third : 2 * third], near[2 * third :])

    for c in range(CHUNKS):
        @pl.when(has_up)
        def _():
            for a in range(2):
                lat_copy(a, 0, c).start()

        @pl.when(has_down)
        def _():
            for a in range(2):
                lat_copy(a, 1, c).start()

        for a in range(2):
            for way in range(2):
                lon_copy(a, 1, way, c).start()

        if c == 0:
            for d in near:
                w1_copy(0, d).start()
        else:
            for d in thirds[c - 1]:
                w1_copy(1, d).start()

    pad_rows = kbuf.shape[0] - 3 * seg
    for ref in (kbuf, vbuf):
        ref[pl.ds(3 * seg, pad_rows), :] = jnp.zeros((pad_rows, width), jnp.bfloat16)

        @pl.when(jnp.logical_not(has_down))
        def _():
            ref[pl.ds(0, seg), :] = jnp.zeros((seg, width), jnp.bfloat16)

        @pl.when(jnp.logical_not(has_up))
        def _():
            ref[pl.ds(2 * seg, seg), :] = jnp.zeros((seg, width), jnp.bfloat16)

    for ref in (gk, gv):
        pad = ref.shape[0] - (STEPS + 1) * tokens
        ref[pl.ds((STEPS + 1) * tokens, pad), :] = jnp.zeros((pad, width), jnp.bfloat16)

    lanes = kbuf.shape[0]
    own_copies[4].wait()
    flat = b_ref[...]
    row_id = lax.broadcasted_iota(jnp.int32, flat.shape, 0)
    shifted = jnp.zeros_like(flat)
    for r in range(8):
        shifted = jnp.where(lax.rem(row_id, 8) == r, pltpu.roll(flat, r + 2, 1), shifted)
    lane = lax.broadcasted_iota(jnp.int32, (flat.shape[1], lanes), 1)
    spot = lax.broadcasted_iota(jnp.int32, (flat.shape[1], lanes), 0)
    at_seg = (lane >= seg).astype(jnp.int32) + (lane >= 2 * seg).astype(jnp.int32)
    inner = lane - at_seg * seg
    wanted = lax.shift_right_logical(inner, 3) * 24 + at_seg * 8 + (inner & 7)
    pick = jnp.where(spot == wanted, 1.0, 0.0).astype(jnp.bfloat16)
    first = shifted.astype(jnp.bfloat16)
    rest = shifted - first.astype(jnp.float32)
    second = rest.astype(jnp.bfloat16)
    third = (rest - second.astype(jnp.float32)).astype(jnp.bfloat16)
    bias = jnp.dot(first, pick, preferred_element_type=jnp.float32)
    bias = bias + jnp.dot(second, pick, preferred_element_type=jnp.float32)
    bias = bias + jnp.dot(third, pick, preferred_element_type=jnp.float32)
    lane = lax.broadcasted_iota(jnp.int32, bias.shape, 1)
    jrow = lax.rem(lax.broadcasted_iota(jnp.int32, bias.shape, 0), 8)
    at_seg = (lane >= seg).astype(jnp.int32) + (lane >= 2 * seg).astype(jnp.int32)
    inner = lane - at_seg * seg
    index = at_seg * 8 + (inner & 7) - jrow - 2
    low_lane = jnp.where(has_down, 0, seg)
    high_lane = jnp.where(has_up, 3 * seg, 2 * seg)
    fits = (inner < 13 * 8) & (index >= 0) & (index < 13) & (lane >= low_lane) & (lane < high_lane)
    rbuf[...] = jnp.where(fits, bias, NEG)

    def forward(c):
        @pl.when(has_down)
        def _():
            for a in range(2):
                lat_copy(a, 0, c).wait_recv()
                for way in range(2):
                    lon_copy(a, 0, way, c).start()

        @pl.when(has_up)
        def _():
            for a in range(2):
                lat_copy(a, 1, c).wait_recv()
                for way in range(2):
                    lon_copy(a, 2, way, c).start()

    def landed(c):
        for a in range(2):
            for way in range(2):
                lon_copy(a, 1, way, c).wait_recv()

        @pl.when(has_down)
        def _():
            for a in range(2):
                for way in range(2):
                    lon_copy(a, 0, way, c).wait_recv()

        @pl.when(has_up)
        def _():
            for a in range(2):
                for way in range(2):
                    lon_copy(a, 2, way, c).wait_recv()

    left = (lax.broadcasted_iota(jnp.int32, (tokens, 128), 1) < 64).astype(jnp.float32)
    left_mask = left.astype(jnp.bfloat16)
    right_mask = (1.0 - left).astype(jnp.bfloat16)

    def two_heads(q2, k2, v2, fix):
        qq = jnp.concatenate([q2 * left_mask, q2 * right_mask], axis=0)
        s = lax.dot_general(qq, k2, (((1,), (1,)), ((), ())), preferred_element_type=jnp.float32)
        s = fix(s * 0.125)
        e = jnp.exp(s - jnp.max(s, axis=1, keepdims=True))
        t = jnp.sum(e, axis=1, keepdims=True)
        o = jnp.dot(e.astype(jnp.bfloat16), v2, preferred_element_type=jnp.float32) / t
        return jnp.where(left > 0.5, o[:tokens], o[tokens:]).astype(jnp.bfloat16)

    def local_pair(h):
        at = pl.ds(pl.multiple_of(h * 128, 128), 128)

        def fix(s):
            parts = []
            for head in range(2):
                r = rbuf[pl.ds(pl.multiple_of(h * 16 + head * 8, 8), 8), :]
                for col in range(tokens // 8):
                    parts.append(r if col == 0 else pltpu.roll(r, col * 8, 1))
            return s + jnp.concatenate(parts, axis=0)

        lo[:, at] = two_heads(q_ref[:, at], kbuf[:, at], vbuf[:, at], fix)

    per = cw // 128
    forward(0)
    spread(0, near)
    forward(1)
    spread(1, thirds[0])
    own_copies[5].wait()
    for copy in own_copies[:2]:
        copy.wait()
    for c in range(CHUNKS):
        landed(c)
        pl.loop(c * per, (c + 1) * per)(local_pair)
        if c < 2:
            forward(c + 2)
            spread(1, thirds[c + 1])
        if c == 0:
            relay(0, near)
        if c == 1:
            corner(0, near)
        if c > 1:
            relay(1, thirds[c - 2])
    own_copies[6].wait()
    own_copies[7].wait()
    gathered(0)

    projected = jnp.dot(lo[...], wo[...], preferred_element_type=jnp.float32)
    hidden = (tok_ref[...].astype(jnp.float32) + projected).astype(jnp.bfloat16)
    hid_ref[...] = hidden
    wide = hidden.astype(jnp.float32)
    inverse = lax.rsqrt(jnp.mean(wide * wide, axis=1, keepdims=True) + 1e-06)
    nbuf[pl.ds(0, tokens), :] = (wide * inverse * gain_ref[...]).astype(jnp.bfloat16)

    def ex_copy(s):
        return rc(
            nbuf.at[pl.ds(0, tokens)],
            nbuf.at[pl.ds(s * tokens, tokens)],
            ex_s.at[s],
            ex_r.at[s],
            line_dev(s),
        )

    for s in range(1, STEPS + 1):
        ex_copy(s).start()
    relay(1, thirds[2])
    for some in thirds:
        corner(1, some)
    gathered(1)

    tile = 512

    def project(at, count, column):
        left_rows = nbuf[pl.ds(at, count), :]
        weight = wg[:, pl.ds(pl.multiple_of(column, tile), tile)]
        return jnp.dot(left_rows, weight, preferred_element_type=jnp.float32).astype(jnp.bfloat16)

    def keys_values(at, count):
        @pl.loop(0, width // tile)
        def _(t):
            here = pl.ds(pl.multiple_of(t * tile, tile), tile)
            gk[pl.ds(at, count), here] = project(at, count, width + t * tile)
            gv[pl.ds(at, count), here] = project(at, count, 2 * width + t * tile)

    @pl.loop(0, width // tile)
    def _(t):
        here = pl.ds(pl.multiple_of(t * tile, tile), tile)
        gq[:, here] = project(0, tokens, t * tile)

    for s in range(1, STEPS + 1):
        ex_copy(s).wait_recv()
    keys_values(0, (STEPS + 1) * tokens)

    def global_pair(h):
        at = pl.ds(pl.multiple_of(h * 128, 128), 128)

        def fix(s):
            key = lax.broadcasted_iota(jnp.int32, s.shape, 1)
            return jnp.where(key < (STEPS + 1) * tokens, s, NEG)

        att_ref[:, at] = two_heads(gq[:, at], gk[:, at], gv[:, at], fix)

    pl.loop(0, width // 128)(global_pair)

    for c in range(CHUNKS):
        for a in range(2):
            for way in range(2):
                lon_copy(a, 1, way, c).wait_send()

        @pl.when(has_up)
        def _():
            for a in range(2):
                lat_copy(a, 0, c).wait_send()
                for way in range(2):
                    lon_copy(a, 2, way, c).wait_send()

        @pl.when(has_down)
        def _():
            for a in range(2):
                lat_copy(a, 1, c).wait_send()
                for way in range(2):
                    lon_copy(a, 0, way, c).wait_send()

    for a in range(2):
        for d in range(1, n_lat):
            w1_copy(a, d).wait_send()
            wp_copy(a, d, j).wait_send()
            for e in range(dims):
                wx_copy(a, d, e, j).wait_send()
                if corners:
                    wh_copy(a, d, e, across(j, e)).wait_send()
            for e in range(dims + corners):
                wm_copy(a, d, e, across(j, e)).wait_send()
    for s in range(1, STEPS + 1):
        ex_copy(s).wait_send()


def body(tokens, query_local, key_local, value_local, position_bias, output_weight, norm_gain, global_weight):
    n_lon = lax.axis_size("lon")
    n_lat = lax.axis_size("lat")
    lon_cells, lat_cells, width = tokens.shape
    count = lon_cells * lat_cells
    heads, window, _ = position_bias.shape
    rows = output_weight.shape[0]
    pieces = min(n_lon, 8 if rows >= 256 else 4)

    def flat(x):
        return x.reshape(count, width)

    table = jnp.pad(position_bias, ((0, 0), (0, 0), (0, 24 - window))).reshape(heads, window * 24)
    table = jnp.pad(table, ((0, 0), (0, 384 - window * 24)))
    table = jnp.broadcast_to(table[:, None, :], (heads, 8, 384)).reshape(heads * 8, 384)
    lanes = -(-(6 * count) // 128) * 128
    keys = -(-((STEPS + 1) * count) // 128) * 128
    vmem = pl.BlockSpec(memory_space=pltpu.VMEM)
    hbm = pl.BlockSpec(memory_space=pltpu.HBM)
    dma = pltpu.SemaphoreType.DMA
    bf16 = jnp.bfloat16
    hidden, attended = pl.pallas_call(
        functools.partial(kernel, n_lon, n_lat, pieces),
        out_shape=(jax.ShapeDtypeStruct((count, width), bf16),) * 2,
        in_specs=[hbm] * 8,
        out_specs=(vmem, vmem),
        scratch_shapes=[
            pltpu.VMEM((count, width), bf16),
            pltpu.VMEM((count, width), bf16),
            pltpu.VMEM((heads * 8, 384), jnp.float32),
            pltpu.VMEM((1, width), jnp.float32),
            pltpu.VMEM((lanes, width), bf16),
            pltpu.VMEM((lanes, width), bf16),
            pltpu.VMEM((width, width), bf16),
            pltpu.VMEM((width, 3 * width), bf16),
            pltpu.VMEM((heads * 8, lanes), jnp.float32),
            pltpu.VMEM((count, width), bf16),
            pltpu.VMEM(((STEPS + 1) * count, width), bf16),
            pltpu.VMEM((count, width), bf16),
            pltpu.VMEM((keys, width), bf16),
            pltpu.VMEM((keys, width), bf16),
            dma((8,)),
            dma((2, 2, CHUNKS)),
            dma((2, 2, CHUNKS)),
            dma((2, 3, 2, CHUNKS)),
            dma((2, 3, 2, CHUNKS)),
            dma((2, n_lat)),
            dma((2, n_lat)),
            dma((2, n_lat)),
            dma((2, n_lat)),
            dma((2, n_lat, 2)),
            dma((2, n_lat, 2)),
            dma((2, n_lat, 2)),
            dma((2, n_lat, 2)),
            dma((2, n_lat, 3)),
            dma((2, n_lat, 3)),
            dma((STEPS + 1,)),
            dma((STEPS + 1,)),
        ],
        compiler_params=pltpu.CompilerParams(
            collective_id=0, has_side_effects=True, vmem_limit_bytes=60 * 1024 * 1024
        ),
    )(
        flat(tokens),
        flat(query_local),
        flat(key_local),
        flat(value_local),
        table,
        output_weight,
        norm_gain.reshape(1, width),
        global_weight,
    )
    return hidden.reshape(tokens.shape), attended.reshape(tokens.shape)


def solution(mesh):
    return jax.shard_map(
        body,
        mesh=mesh,
        in_specs=(
            P("lon", "lat", None),
            P("lon", "lat", None),
            P("lon", "lat", None),
            P("lon", "lat", None),
            P(),
            P("lat", None),
            P(),
            P("lat", None),
        ),
        out_specs=(P("lon", "lat", None), P("lon", "lat", None)),
        check_vma=False,
    )
```

```python
import functools

import jax
import jax.numpy as jnp
from jax import lax
from jax.experimental import pallas as pl
from jax.experimental.pallas import tpu as pltpu
from jax.sharding import PartitionSpec as P

STEPS = 4
CHUNKS = 4
NEG = -1e30
MESH = pl.DeviceIdType.MESH


def kernel(
    n_lon,
    n_lat,
    pieces,
    tok_hbm,
    q_hbm,
    k_hbm,
    v_hbm,
    b_hbm,
    wo_hbm,
    gain_hbm,
    wg_hbm,
    hid_ref,
    att_ref,
    tok_ref,
    q_ref,
    b_ref,
    gain_ref,
    kbuf,
    vbuf,
    wo,
    wg,
    rbuf,
    lo,
    nbuf,
    gq,
    gk,
    gv,
    own_sem,
    lat_s,
    lat_r,
    lon_s,
    lon_r,
    w1_s,
    w1_r,
    wp_s,
    wp_r,
    wx_s,
    wx_r,
    wh_s,
    wh_r,
    wm_s,
    wm_r,
    ex_s,
    ex_r,
):
    i = lax.axis_index("lon")
    z = lax.axis_index("lat")
    rows = wo_hbm.shape[0]
    part = rows // pieces
    tokens, width = tok_ref.shape
    half = tokens // 2
    seg = 2 * tokens
    cw = width // CHUNKS
    j = lax.rem(i, pieces)
    base = i - j
    dims = pieces.bit_length() - 2

    def flip(at, bit):
        return at + bit - 2 * bit * lax.rem(at // bit, 2)

    mate = base + flip(j, 1)
    p = i * n_lat + z
    total = n_lon * n_lat

    def lat_dev(d):
        return (i, lax.rem(z + d + n_lat, n_lat))

    def lon_dev(d):
        return (lax.rem(i + d + n_lon, n_lon), z)

    def side(e):
        return (base + flip(j, 2 << e), z)

    def line_dev(s):
        t = lax.rem(p + s + total, total)
        return (t // n_lat, lax.rem(t, n_lat))

    def rc(src, dst, ssem, rsem, dev):
        return pltpu.make_async_remote_copy(
            src_ref=src, dst_ref=dst, send_sem=ssem, recv_sem=rsem, device_id=dev, device_id_type=MESH
        )

    barrier = pltpu.get_barrier_semaphore()
    greet = [lat_dev(1), lat_dev(-1)]
    greet += [lon_dev(1), lon_dev(-1), (mate, z)]
    greet += [side(e) for e in range(dims)]
    greet += [line_dev(-s) for s in range(1, STEPS + 1)]
    for dev in greet:
        pl.semaphore_signal(barrier, inc=1, device_id=dev, device_id_type=MESH)

    pairs = ((k_hbm, kbuf), (v_hbm, vbuf))
    weights = ((wo_hbm, wo), (wg_hbm, wg))
    own_copies = []
    for a, (src, dst) in enumerate(pairs):
        own_copies.append(
            pltpu.make_async_copy(src, dst.at[pl.ds(seg + half, tokens)], own_sem.at[a])
        )
    for a, (src, dst) in enumerate(weights):
        own_copies.append(
            pltpu.make_async_copy(
                src, dst.at[pl.ds(pl.multiple_of(z * rows, 16), rows)], own_sem.at[2 + a]
            )
        )
    singles = ((b_hbm, b_ref), (q_hbm, q_ref), (tok_hbm, tok_ref), (gain_hbm, gain_ref))
    for a, (src, dst) in enumerate(singles):
        own_copies.append(pltpu.make_async_copy(src, dst, own_sem.at[4 + a]))
    for at in (4, 0, 1, 5, 2, 3, 6, 7):
        own_copies[at].start()
    pl.semaphore_wait(barrier, len(greet))

    def cols(c):
        return pl.ds(c * cw, cw)

    def lat_copy(a, way, c):
        src, dst = pairs[a]
        at = 0 if way == 0 else 2
        return rc(
            src.at[:, cols(c)],
            dst.at[pl.ds(at * seg + half, tokens), cols(c)],
            lat_s.at[a, way, c],
            lat_r.at[a, way, c],
            lat_dev(1 if way == 0 else -1),
        )

    def lon_copy(a, s, way, c):
        src, dst = pairs[a]
        if s == 1:
            source = src.at[pl.ds(half if way == 0 else 0, half), cols(c)]
        else:
            source = dst.at[pl.ds(s * seg + (tokens if way == 0 else half), half), cols(c)]
        return rc(
            source,
            dst.at[pl.ds(s * seg + (0 if way == 0 else half + tokens), half), cols(c)],
            lon_s.at[a, s, way, c],
            lon_r.at[a, s, way, c],
            lon_dev(1 if way == 0 else -1),
        )

    has_up = z < n_lat - 1
    has_down = z > 0

    routes = [(way, d) for d in range(1, n_lat) for way in (1, -1)]

    def shard_of(way, d):
        return z - way * d

    def exists(way, d):
        return (shard_of(way, d) >= 0) & (shard_of(way, d) < n_lat)

    def w_rows(shard, piece):
        return pl.ds(pl.multiple_of(shard * rows + piece * part, 16), part)

    def w_move(a, shard, piece, ssem, rsem, dev):
        ref = weights[a][1].at[w_rows(shard, piece)]
        return rc(ref, ref, ssem, rsem, dev)

    def w1_copy(a, way, d):
        shard = shard_of(way, d - 1)
        sems = (w1_s.at[a, max(way, 0), d], w1_r.at[a, max(way, 0), d])
        if d > 1:
            return w_move(a, shard, j, *sems, lat_dev(way))
        src, dst = weights[a]
        piece = src.at[pl.ds(pl.multiple_of(j * part, 16), part)]
        return rc(piece, dst.at[w_rows(z, j)], *sems, lat_dev(way))

    def w1_wait(a, way, d):
        sems = (w1_s.at[a, max(way, 0), d], w1_r.at[a, max(way, 0), d])
        w_move(a, shard_of(way, d), j, *sems, lat_dev(way)).wait_recv()

    def onward(way, d):
        return exists(way, d - 1) & (has_up if way > 0 else has_down)

    def wp_copy(a, t, piece):
        return w_move(a, t, piece, wp_s.at[a, t], wp_r.at[a, t], (mate, z))

    def w_half(a, t, piece, e, ssem, rsem, dev):
        size = part // 2
        at = t * rows + piece * part + e * size
        ref = weights[a][1].at[pl.ds(pl.multiple_of(at, 16), size)]
        return rc(ref, ref, ssem, rsem, dev)

    def wx_copy(a, t, e, piece):
        return w_move(a, t, piece, wx_s.at[a, t, e], wx_r.at[a, t, e], side(e))

    def wh_copy(a, t, e, piece):
        return w_half(a, t, piece, e, wh_s.at[a, t, e], wh_r.at[a, t, e], side(1 - e))

    def wm_copy(a, t, e, piece):
        return w_move(a, t, piece, wm_s.at[a, t, e], wm_r.at[a, t, e], (mate, z))

    mate_piece = flip(j, 1)
    corners = 1 if dims == 2 else 0

    def across(at, e):
        return flip(at, 2 << e) if e < 2 else flip(flip(at, 2), 4)

    def each(ds, step):
        for way, d in routes:
            if d in ds:
                pl.when(exists(way, d))(functools.partial(step, way, d))

    def spread(a, ds):
        def step(way, d):
            w1_wait(a, way, d)
            if d + 1 < n_lat:
                pl.when(onward(way, d + 1))(lambda: w1_copy(a, way, d + 1).start())
            t = shard_of(way, d)
            for e in range(dims):
                wx_copy(a, t, e, j).start()
            wp_copy(a, t, j).start()

        each(ds, step)

    def relay(a, ds):
        def step(way, d):
            t = shard_of(way, d)
            for e in range(dims):
                piece = across(j, e)
                wx_copy(a, t, e, piece).wait_recv()
                if corners:
                    wh_copy(a, t, e, piece).start()
                wm_copy(a, t, e, piece).start()

        each(ds, step)

    def corner(a, ds):
        def step(way, d):
            t = shard_of(way, d)
            piece = across(j, 2)
            for e in range(2):
                wh_copy(a, t, e, piece).wait_recv()
            wm_copy(a, t, 2, piece).start()

        if corners:
            each(ds, step)

    def gathered(a):
        def step(way, d):
            t = shard_of(way, d)
            wp_copy(a, t, mate_piece).wait_recv()
            for e in range(dims + corners):
                wm_copy(a, t, e, across(mate_piece, e)).wait_recv()

        own_copies[2 + a].wait()
        each(range(1, n_lat), step)

    one, two, three = (1,), (2,), tuple(range(3, n_lat))

    for c in range(CHUNKS):
        @pl.when(has_up)
        def _():
            for a in range(2):
                lat_copy(a, 0, c).start()

        @pl.when(has_down)
        def _():
            for a in range(2):
                lat_copy(a, 1, c).start()

        for a in range(2):
            for way in range(2):
                lon_copy(a, 1, way, c).start()

    for a in range(2):
        for way in (1, -1):
            pl.when(onward(way, 1))(lambda: w1_copy(a, way, 1).start())

    pad_rows = kbuf.shape[0] - 3 * seg
    for ref in (kbuf, vbuf):
        ref[pl.ds(3 * seg, pad_rows), :] = jnp.zeros((pad_rows, width), jnp.bfloat16)

        @pl.when(jnp.logical_not(has_down))
        def _():
            ref[pl.ds(0, seg), :] = jnp.zeros((seg, width), jnp.bfloat16)

        @pl.when(jnp.logical_not(has_up))
        def _():
            ref[pl.ds(2 * seg, seg), :] = jnp.zeros((seg, width), jnp.bfloat16)

    for ref in (gk, gv):
        pad = ref.shape[0] - (STEPS + 1) * tokens
        ref[pl.ds((STEPS + 1) * tokens, pad), :] = jnp.zeros((pad, width), jnp.bfloat16)

    lanes = kbuf.shape[0]
    own_copies[4].wait()
    flat = b_ref[...]
    row_id = lax.broadcasted_iota(jnp.int32, flat.shape, 0)
    shifted = jnp.zeros_like(flat)
    for r in range(8):
        shifted = jnp.where(lax.rem(row_id, 8) == r, pltpu.roll(flat, r + 2, 1), shifted)
    lane = lax.broadcasted_iota(jnp.int32, (flat.shape[1], lanes), 1)
    spot = lax.broadcasted_iota(jnp.int32, (flat.shape[1], lanes), 0)
    at_seg = (lane >= seg).astype(jnp.int32) + (lane >= 2 * seg).astype(jnp.int32)
    inner = lane - at_seg * seg
    wanted = lax.shift_right_logical(inner, 3) * 24 + at_seg * 8 + (inner & 7)
    pick = jnp.where(spot == wanted, 1.0, 0.0).astype(jnp.bfloat16)
    first = shifted.astype(jnp.bfloat16)
    rest = shifted - first.astype(jnp.float32)
    second = rest.astype(jnp.bfloat16)
    third = (rest - second.astype(jnp.float32)).astype(jnp.bfloat16)
    bias = jnp.dot(first, pick, preferred_element_type=jnp.float32)
    bias = bias + jnp.dot(second, pick, preferred_element_type=jnp.float32)
    bias = bias + jnp.dot(third, pick, preferred_element_type=jnp.float32)
    lane = lax.broadcasted_iota(jnp.int32, bias.shape, 1)
    jrow = lax.rem(lax.broadcasted_iota(jnp.int32, bias.shape, 0), 8)
    at_seg = (lane >= seg).astype(jnp.int32) + (lane >= 2 * seg).astype(jnp.int32)
    inner = lane - at_seg * seg
    index = at_seg * 8 + (inner & 7) - jrow - 2
    low_lane = jnp.where(has_down, 0, seg)
    high_lane = jnp.where(has_up, 3 * seg, 2 * seg)
    fits = (inner < 13 * 8) & (index >= 0) & (index < 13) & (lane >= low_lane) & (lane < high_lane)
    rbuf[...] = jnp.where(fits, bias, NEG)

    def forward(c):
        @pl.when(has_down)
        def _():
            for a in range(2):
                lat_copy(a, 0, c).wait_recv()
                for way in range(2):
                    lon_copy(a, 0, way, c).start()

        @pl.when(has_up)
        def _():
            for a in range(2):
                lat_copy(a, 1, c).wait_recv()
                for way in range(2):
                    lon_copy(a, 2, way, c).start()

    def landed(c):
        for a in range(2):
            for way in range(2):
                lon_copy(a, 1, way, c).wait_recv()

        @pl.when(has_down)
        def _():
            for a in range(2):
                for way in range(2):
                    lon_copy(a, 0, way, c).wait_recv()

        @pl.when(has_up)
        def _():
            for a in range(2):
                for way in range(2):
                    lon_copy(a, 2, way, c).wait_recv()

    left = (lax.broadcasted_iota(jnp.int32, (tokens, 128), 1) < 64).astype(jnp.float32)
    left_mask = left.astype(jnp.bfloat16)
    right_mask = (1.0 - left).astype(jnp.bfloat16)

    def two_heads(q2, k2, v2, fix):
        qq = jnp.concatenate([q2 * left_mask, q2 * right_mask], axis=0)
        s = lax.dot_general(qq, k2, (((1,), (1,)), ((), ())), preferred_element_type=jnp.float32)
        s = fix(s * 0.125)
        e = jnp.exp(s - jnp.max(s, axis=1, keepdims=True))
        t = jnp.sum(e, axis=1, keepdims=True)
        o = jnp.dot(e.astype(jnp.bfloat16), v2, preferred_element_type=jnp.float32) / t
        return jnp.where(left > 0.5, o[:tokens], o[tokens:]).astype(jnp.bfloat16)

    def local_pair(h):
        at = pl.ds(pl.multiple_of(h * 128, 128), 128)

        def fix(s):
            parts = []
            for head in range(2):
                r = rbuf[pl.ds(pl.multiple_of(h * 16 + head * 8, 8), 8), :]
                for col in range(tokens // 8):
                    parts.append(r if col == 0 else pltpu.roll(r, col * 8, 1))
            return s + jnp.concatenate(parts, axis=0)

        lo[:, at] = two_heads(q_ref[:, at], kbuf[:, at], vbuf[:, at], fix)

    per = cw // 128
    for c in range(CHUNKS):
        forward(c)
    spread(0, one)
    own_copies[5].wait()
    for copy in own_copies[:2]:
        copy.wait()
    for c in range(CHUNKS):
        landed(c)
        pl.loop(c * per, (c + 1) * per)(local_pair)
        if c == 0:
            spread(0, two)
            relay(0, one)
        if c == 1:
            spread(1, one)
            spread(0, three)
            relay(0, two)
        if c == 2:
            spread(1, two)
            relay(0, three)
            corner(0, one + two)
    corner(0, three)
    relay(1, one)
    own_copies[6].wait()
    own_copies[7].wait()
    gathered(0)

    projected = jnp.dot(lo[...], wo[...], preferred_element_type=jnp.float32)
    hidden = (tok_ref[...].astype(jnp.float32) + projected).astype(jnp.bfloat16)
    hid_ref[...] = hidden
    wide = hidden.astype(jnp.float32)
    inverse = lax.rsqrt(jnp.mean(wide * wide, axis=1, keepdims=True) + 1e-06)
    nbuf[pl.ds(0, tokens), :] = (wide * inverse * gain_ref[...]).astype(jnp.bfloat16)

    def block(s):
        return nbuf.at[pl.ds(s * tokens, tokens)]

    def ex_copy(s):
        return rc(block(0), block(s), ex_s.at[s], ex_r.at[s], line_dev(s))

    staged = n_lat == 4

    def direct(s, act):
        if staged and s == 3:
            pl.when(z != 0)(act)
        elif staged and s == 1:
            pl.when(z != n_lat - 1)(act)
        else:
            act()

    up_copy = rc(block(2), block(3), ex_s.at[0], ex_r.at[3], lat_dev(1))
    down_copy = rc(block(2), block(1), ex_s.at[0], ex_r.at[1], lat_dev(-1))

    for s in (2, 3, 1, 4):
        direct(s, lambda: ex_copy(s).start())
    spread(1, three)
    relay(1, two)
    corner(1, one)
    ex_copy(2).wait_recv()
    if staged:
        pl.when(z == 2)(lambda: up_copy.start())
        pl.when(z == 1)(lambda: down_copy.start())
    relay(1, three)
    corner(1, two)
    corner(1, three)
    gathered(1)

    tile = 512

    def project(at, count, column):
        left_rows = nbuf[pl.ds(at, count), :]
        weight = wg[:, pl.ds(pl.multiple_of(column, tile), tile)]
        return jnp.dot(left_rows, weight, preferred_element_type=jnp.float32).astype(jnp.bfloat16)

    def keys_values(at, count):
        @pl.loop(0, width // tile)
        def _(t):
            here = pl.ds(pl.multiple_of(t * tile, tile), tile)
            gk[pl.ds(at, count), here] = project(at, count, width + t * tile)
            gv[pl.ds(at, count), here] = project(at, count, 2 * width + t * tile)

    @pl.loop(0, width // tile)
    def _(t):
        here = pl.ds(pl.multiple_of(t * tile, tile), tile)
        gq[:, here] = project(0, tokens, t * tile)

    for s in (1, 3, 4):
        ex_copy(s).wait_recv()
    keys_values(0, (STEPS + 1) * tokens)

    def global_pair(h):
        at = pl.ds(pl.multiple_of(h * 128, 128), 128)

        def fix(s):
            key = lax.broadcasted_iota(jnp.int32, s.shape, 1)
            return jnp.where(key < (STEPS + 1) * tokens, s, NEG)

        att_ref[:, at] = two_heads(gq[:, at], gk[:, at], gv[:, at], fix)

    pl.loop(0, width // 128)(global_pair)

    for c in range(CHUNKS):
        for a in range(2):
            for way in range(2):
                lon_copy(a, 1, way, c).wait_send()

        @pl.when(has_up)
        def _():
            for a in range(2):
                lat_copy(a, 0, c).wait_send()
                for way in range(2):
                    lon_copy(a, 2, way, c).wait_send()

        @pl.when(has_down)
        def _():
            for a in range(2):
                lat_copy(a, 1, c).wait_send()
                for way in range(2):
                    lon_copy(a, 0, way, c).wait_send()

    for a in range(2):
        def sent(way, d):
            t = shard_of(way, d)
            wp_copy(a, t, j).wait_send()
            for e in range(dims):
                wx_copy(a, t, e, j).wait_send()
                if corners:
                    wh_copy(a, t, e, across(j, e)).wait_send()
            for e in range(dims + corners):
                wm_copy(a, t, e, across(j, e)).wait_send()

        each(range(1, n_lat), sent)
        for way, d in routes:
            pl.when(onward(way, d))(lambda: w1_copy(a, way, d).wait_send())
    for s in range(1, STEPS + 1):
        direct(s, lambda: ex_copy(s).wait_send())
    if staged:
        pl.when(z == 2)(lambda: up_copy.wait_send())
        pl.when(z == 1)(lambda: down_copy.wait_send())


def body(tokens, query_local, key_local, value_local, position_bias, output_weight, norm_gain, global_weight):
    n_lon = lax.axis_size("lon")
    n_lat = lax.axis_size("lat")
    lon_cells, lat_cells, width = tokens.shape
    count = lon_cells * lat_cells
    heads, window, _ = position_bias.shape
    rows = output_weight.shape[0]
    pieces = min(n_lon, 8 if rows >= 256 else 4)

    def flat(x):
        return x.reshape(count, width)

    table = jnp.pad(position_bias, ((0, 0), (0, 0), (0, 24 - window))).reshape(heads, window * 24)
    table = jnp.pad(table, ((0, 0), (0, 384 - window * 24)))
    table = jnp.broadcast_to(table[:, None, :], (heads, 8, 384)).reshape(heads * 8, 384)
    lanes = -(-(6 * count) // 128) * 128
    keys = -(-((STEPS + 1) * count) // 128) * 128
    vmem = pl.BlockSpec(memory_space=pltpu.VMEM)
    hbm = pl.BlockSpec(memory_space=pltpu.HBM)
    dma = pltpu.SemaphoreType.DMA
    bf16 = jnp.bfloat16
    hidden, attended = pl.pallas_call(
        functools.partial(kernel, n_lon, n_lat, pieces),
        out_shape=(jax.ShapeDtypeStruct((count, width), bf16),) * 2,
        in_specs=[hbm] * 8,
        out_specs=(vmem, vmem),
        scratch_shapes=[
            pltpu.VMEM((count, width), bf16),
            pltpu.VMEM((count, width), bf16),
            pltpu.VMEM((heads * 8, 384), jnp.float32),
            pltpu.VMEM((1, width), jnp.float32),
            pltpu.VMEM((lanes, width), bf16),
            pltpu.VMEM((lanes, width), bf16),
            pltpu.VMEM((width, width), bf16),
            pltpu.VMEM((width, 3 * width), bf16),
            pltpu.VMEM((heads * 8, lanes), jnp.float32),
            pltpu.VMEM((count, width), bf16),
            pltpu.VMEM(((STEPS + 1) * count, width), bf16),
            pltpu.VMEM((count, width), bf16),
            pltpu.VMEM((keys, width), bf16),
            pltpu.VMEM((keys, width), bf16),
            dma((8,)),
            dma((2, 2, CHUNKS)),
            dma((2, 2, CHUNKS)),
            dma((2, 3, 2, CHUNKS)),
            dma((2, 3, 2, CHUNKS)),
            dma((2, 2, n_lat)),
            dma((2, 2, n_lat)),
            dma((2, n_lat)),
            dma((2, n_lat)),
            dma((2, n_lat, 2)),
            dma((2, n_lat, 2)),
            dma((2, n_lat, 2)),
            dma((2, n_lat, 2)),
            dma((2, n_lat, 3)),
            dma((2, n_lat, 3)),
            dma((STEPS + 1,)),
            dma((STEPS + 1,)),
        ],
        compiler_params=pltpu.CompilerParams(
            collective_id=0, has_side_effects=True, vmem_limit_bytes=60 * 1024 * 1024
        ),
    )(
        flat(tokens),
        flat(query_local),
        flat(key_local),
        flat(value_local),
        table,
        output_weight,
        norm_gain.reshape(1, width),
        global_weight,
    )
    return hidden.reshape(tokens.shape), attended.reshape(tokens.shape)


def solution(mesh):
    return jax.shard_map(
        body,
        mesh=mesh,
        in_specs=(
            P("lon", "lat", None),
            P("lon", "lat", None),
            P("lon", "lat", None),
            P("lon", "lat", None),
            P(),
            P("lat", None),
            P(),
            P("lat", None),
        ),
        out_specs=(P("lon", "lat", None), P("lon", "lat", None)),
        check_vma=False,
    )
```

```python
import functools

import jax
import jax.numpy as jnp
from jax import lax
from jax.experimental import pallas as pl
from jax.experimental.pallas import tpu as pltpu
from jax.sharding import PartitionSpec as P

STEPS = 4
CHUNKS = 4
NEG = -1e30
MESH = pl.DeviceIdType.MESH


def kernel(
    n_lon,
    n_lat,
    pieces,
    tok_hbm,
    q_hbm,
    k_hbm,
    v_hbm,
    b_hbm,
    wo_hbm,
    gain_hbm,
    wg_hbm,
    hid_ref,
    att_ref,
    tok_ref,
    q_ref,
    b_ref,
    tab,
    gain_ref,
    kbuf,
    vbuf,
    wo,
    wg,
    rbuf,
    lo,
    nbuf,
    gq,
    gk,
    gv,
    own_sem,
    lat_s,
    lat_r,
    lon_s,
    lon_r,
    w1_s,
    w1_r,
    wp_s,
    wp_r,
    wx_s,
    wx_r,
    wh_s,
    wh_r,
    wm_s,
    wm_r,
    ex_s,
    ex_r,
):
    i = lax.axis_index("lon")
    z = lax.axis_index("lat")
    rows = wo_hbm.shape[0]
    part = rows // pieces
    tokens, width = tok_ref.shape
    half = tokens // 2
    seg = 2 * tokens
    cw = width // CHUNKS
    j = lax.rem(i, pieces)
    base = i - j
    dims = pieces.bit_length() - 2

    def flip(at, bit):
        return at + bit - 2 * bit * lax.rem(at // bit, 2)

    mate = base + flip(j, 1)
    p = i * n_lat + z
    total = n_lon * n_lat

    def lat_dev(d):
        return (i, lax.rem(z + d + n_lat, n_lat))

    def lon_dev(d):
        return (lax.rem(i + d + n_lon, n_lon), z)

    def side(e):
        return (base + flip(j, 2 << e), z)

    def line_dev(s):
        t = lax.rem(p + s + total, total)
        return (t // n_lat, lax.rem(t, n_lat))

    def rc(src, dst, ssem, rsem, dev):
        return pltpu.make_async_remote_copy(
            src_ref=src, dst_ref=dst, send_sem=ssem, recv_sem=rsem, device_id=dev, device_id_type=MESH
        )

    barrier = pltpu.get_barrier_semaphore()
    greet = [lat_dev(1), lat_dev(-1)]
    greet += [lon_dev(1), lon_dev(-1), (mate, z)]
    greet += [side(e) for e in range(dims)]
    greet += [line_dev(-s) for s in range(1, STEPS + 1)]
    for dev in greet:
        pl.semaphore_signal(barrier, inc=1, device_id=dev, device_id_type=MESH)

    pairs = ((k_hbm, kbuf), (v_hbm, vbuf))
    weights = ((wo_hbm, wo), (wg_hbm, wg))
    own_copies = []
    for a, (src, dst) in enumerate(pairs):
        own_copies.append(
            pltpu.make_async_copy(src, dst.at[pl.ds(seg + half, tokens)], own_sem.at[a])
        )
    for a, (src, dst) in enumerate(weights):
        own_copies.append(
            pltpu.make_async_copy(
                src, dst.at[pl.ds(pl.multiple_of(z * rows, 16), rows)], own_sem.at[2 + a]
            )
        )
    singles = ((b_hbm, b_ref), (q_hbm, q_ref), (tok_hbm, tok_ref), (gain_hbm, gain_ref))
    for a, (src, dst) in enumerate(singles):
        own_copies.append(pltpu.make_async_copy(src, dst, own_sem.at[4 + a]))
    for at in (4, 0, 1, 5, 2, 3, 6, 7):
        own_copies[at].start()
    pl.semaphore_wait(barrier, len(greet))

    def cols(c):
        return pl.ds(c * cw, cw)

    def lat_copy(a, way, c):
        src, dst = pairs[a]
        at = 0 if way == 0 else 2
        return rc(
            src.at[:, cols(c)],
            dst.at[pl.ds(at * seg + half, tokens), cols(c)],
            lat_s.at[a, way, c],
            lat_r.at[a, way, c],
            lat_dev(1 if way == 0 else -1),
        )

    def lon_copy(a, s, way, c):
        src, dst = pairs[a]
        if s == 1:
            source = src.at[pl.ds(half if way == 0 else 0, half), cols(c)]
        else:
            source = dst.at[pl.ds(s * seg + (tokens if way == 0 else half), half), cols(c)]
        return rc(
            source,
            dst.at[pl.ds(s * seg + (0 if way == 0 else half + tokens), half), cols(c)],
            lon_s.at[a, s, way, c],
            lon_r.at[a, s, way, c],
            lon_dev(1 if way == 0 else -1),
        )

    has_up = z < n_lat - 1
    has_down = z > 0

    routes = [(way, d) for d in range(1, n_lat) for way in (1, -1)]

    def shard_of(way, d):
        return z - way * d

    def exists(way, d):
        return (shard_of(way, d) >= 0) & (shard_of(way, d) < n_lat)

    def w_rows(shard, piece):
        return pl.ds(pl.multiple_of(shard * rows + piece * part, 16), part)

    def w_move(a, shard, piece, ssem, rsem, dev):
        ref = weights[a][1].at[w_rows(shard, piece)]
        return rc(ref, ref, ssem, rsem, dev)

    def w1_copy(a, way, d):
        shard = shard_of(way, d - 1)
        sems = (w1_s.at[a, max(way, 0), d], w1_r.at[a, max(way, 0), d])
        if d > 1:
            return w_move(a, shard, j, *sems, lat_dev(way))
        src, dst = weights[a]
        piece = src.at[pl.ds(pl.multiple_of(j * part, 16), part)]
        return rc(piece, dst.at[w_rows(z, j)], *sems, lat_dev(way))

    def w1_wait(a, way, d):
        sems = (w1_s.at[a, max(way, 0), d], w1_r.at[a, max(way, 0), d])
        w_move(a, shard_of(way, d), j, *sems, lat_dev(way)).wait_recv()

    def onward(way, d):
        return exists(way, d - 1) & (has_up if way > 0 else has_down)

    def wp_copy(a, t, piece):
        return w_move(a, t, piece, wp_s.at[a, t], wp_r.at[a, t], (mate, z))

    def w_half(a, t, piece, e, ssem, rsem, dev):
        size = part // 2
        at = t * rows + piece * part + e * size
        ref = weights[a][1].at[pl.ds(pl.multiple_of(at, 16), size)]
        return rc(ref, ref, ssem, rsem, dev)

    def wx_copy(a, t, e, piece):
        return w_move(a, t, piece, wx_s.at[a, t, e], wx_r.at[a, t, e], side(e))

    def wh_copy(a, t, e, piece):
        return w_half(a, t, piece, e, wh_s.at[a, t, e], wh_r.at[a, t, e], side(1 - e))

    def wm_copy(a, t, e, piece):
        return w_move(a, t, piece, wm_s.at[a, t, e], wm_r.at[a, t, e], (mate, z))

    mate_piece = flip(j, 1)
    corners = 1 if dims == 2 else 0

    def across(at, e):
        return flip(at, 2 << e) if e < 2 else flip(flip(at, 2), 4)

    def each(ds, step):
        for way, d in routes:
            if d in ds:
                pl.when(exists(way, d))(functools.partial(step, way, d))

    def spread(a, ds):
        def step(way, d):
            w1_wait(a, way, d)
            if d + 1 < n_lat:
                pl.when(onward(way, d + 1))(lambda: w1_copy(a, way, d + 1).start())
            t = shard_of(way, d)
            for e in range(dims):
                wx_copy(a, t, e, j).start()
            wp_copy(a, t, j).start()

        each(ds, step)

    def relay(a, ds):
        def step(way, d):
            t = shard_of(way, d)
            for e in range(dims):
                piece = across(j, e)
                wx_copy(a, t, e, piece).wait_recv()
                if corners:
                    wh_copy(a, t, e, piece).start()
                wm_copy(a, t, e, piece).start()

        each(ds, step)

    def corner(a, ds):
        def step(way, d):
            t = shard_of(way, d)
            piece = across(j, 2)
            for e in range(2):
                wh_copy(a, t, e, piece).wait_recv()
            wm_copy(a, t, 2, piece).start()

        if corners:
            each(ds, step)

    def gathered(a):
        def step(way, d):
            t = shard_of(way, d)
            wp_copy(a, t, mate_piece).wait_recv()
            for e in range(dims + corners):
                wm_copy(a, t, e, across(mate_piece, e)).wait_recv()

        own_copies[2 + a].wait()
        each(range(1, n_lat), step)

    one, two, three = (1,), (2,), tuple(range(3, n_lat))

    for c in range(CHUNKS):
        @pl.when(has_up)
        def _():
            for a in range(2):
                lat_copy(a, 0, c).start()

        @pl.when(has_down)
        def _():
            for a in range(2):
                lat_copy(a, 1, c).start()

        for a in range(2):
            for way in range(2):
                lon_copy(a, 1, way, c).start()

    for a in range(2):
        for way in (1, -1):
            pl.when(onward(way, 1))(lambda: w1_copy(a, way, 1).start())

    pad_rows = kbuf.shape[0] - 3 * seg
    for ref in (kbuf, vbuf):
        ref[pl.ds(3 * seg, pad_rows), :] = jnp.zeros((pad_rows, width), jnp.bfloat16)

        @pl.when(jnp.logical_not(has_down))
        def _():
            ref[pl.ds(0, seg), :] = jnp.zeros((seg, width), jnp.bfloat16)

        @pl.when(jnp.logical_not(has_up))
        def _():
            ref[pl.ds(2 * seg, seg), :] = jnp.zeros((seg, width), jnp.bfloat16)

    for ref in (gk, gv):
        pad = ref.shape[0] - (STEPS + 1) * tokens
        ref[pl.ds((STEPS + 1) * tokens, pad), :] = jnp.zeros((pad, width), jnp.bfloat16)

    lanes = kbuf.shape[0]
    own_copies[4].wait()
    window = b_ref.shape[0]
    tab[...] = jnp.zeros_like(tab)
    for r in range(window):
        tab[:, r * 24 : r * 24 + window] = b_ref[r]
    heads = tab.shape[0]
    flat = jnp.concatenate(
        [jnp.broadcast_to(tab[h : h + 1, :], (8, tab.shape[1])) for h in range(heads)], axis=0
    )
    row_id = lax.broadcasted_iota(jnp.int32, flat.shape, 0)
    shifted = jnp.zeros_like(flat)
    for r in range(8):
        shifted = jnp.where(lax.rem(row_id, 8) == r, pltpu.roll(flat, r + 2, 1), shifted)
    lane = lax.broadcasted_iota(jnp.int32, (flat.shape[1], lanes), 1)
    spot = lax.broadcasted_iota(jnp.int32, (flat.shape[1], lanes), 0)
    at_seg = (lane >= seg).astype(jnp.int32) + (lane >= 2 * seg).astype(jnp.int32)
    inner = lane - at_seg * seg
    wanted = lax.shift_right_logical(inner, 3) * 24 + at_seg * 8 + (inner & 7)
    pick = jnp.where(spot == wanted, 1.0, 0.0).astype(jnp.bfloat16)
    first = shifted.astype(jnp.bfloat16)
    rest = shifted - first.astype(jnp.float32)
    second = rest.astype(jnp.bfloat16)
    third = (rest - second.astype(jnp.float32)).astype(jnp.bfloat16)
    bias = jnp.dot(first, pick, preferred_element_type=jnp.float32)
    bias = bias + jnp.dot(second, pick, preferred_element_type=jnp.float32)
    bias = bias + jnp.dot(third, pick, preferred_element_type=jnp.float32)
    lane = lax.broadcasted_iota(jnp.int32, bias.shape, 1)
    jrow = lax.rem(lax.broadcasted_iota(jnp.int32, bias.shape, 0), 8)
    at_seg = (lane >= seg).astype(jnp.int32) + (lane >= 2 * seg).astype(jnp.int32)
    inner = lane - at_seg * seg
    index = at_seg * 8 + (inner & 7) - jrow - 2
    low_lane = jnp.where(has_down, 0, seg)
    high_lane = jnp.where(has_up, 3 * seg, 2 * seg)
    fits = (inner < 13 * 8) & (index >= 0) & (index < 13) & (lane >= low_lane) & (lane < high_lane)
    rbuf[...] = jnp.where(fits, bias, NEG)

    def forward(c):
        @pl.when(has_down)
        def _():
            for a in range(2):
                lat_copy(a, 0, c).wait_recv()
                for way in range(2):
                    lon_copy(a, 0, way, c).start()

        @pl.when(has_up)
        def _():
            for a in range(2):
                lat_copy(a, 1, c).wait_recv()
                for way in range(2):
                    lon_copy(a, 2, way, c).start()

    def landed(c):
        for a in range(2):
            for way in range(2):
                lon_copy(a, 1, way, c).wait_recv()

        @pl.when(has_down)
        def _():
            for a in range(2):
                for way in range(2):
                    lon_copy(a, 0, way, c).wait_recv()

        @pl.when(has_up)
        def _():
            for a in range(2):
                for way in range(2):
                    lon_copy(a, 2, way, c).wait_recv()

    left = (lax.broadcasted_iota(jnp.int32, (tokens, 128), 1) < 64).astype(jnp.float32)
    left_mask = left.astype(jnp.bfloat16)
    right_mask = (1.0 - left).astype(jnp.bfloat16)

    def two_heads(q2, k2, v2, fix):
        q2 = q2 * jnp.bfloat16(0.125)
        qq = jnp.concatenate([q2 * left_mask, q2 * right_mask], axis=0)
        s = lax.dot_general(qq, k2, (((1,), (1,)), ((), ())), preferred_element_type=jnp.float32)
        s = fix(s)
        e = jnp.exp(s - jnp.max(s, axis=1, keepdims=True))
        t = jnp.sum(e, axis=1, keepdims=True)
        o = jnp.dot(e.astype(jnp.bfloat16), v2, preferred_element_type=jnp.float32) / t
        return jnp.where(left > 0.5, o[:tokens], o[tokens:]).astype(jnp.bfloat16)

    def local_pair(h):
        at = pl.ds(pl.multiple_of(h * 128, 128), 128)

        def fix(s):
            parts = []
            for head in range(2):
                r = rbuf[pl.ds(pl.multiple_of(h * 16 + head * 8, 8), 8), :]
                for col in range(tokens // 8):
                    parts.append(r if col == 0 else pltpu.roll(r, col * 8, 1))
            return s + jnp.concatenate(parts, axis=0)

        lo[:, at] = two_heads(q_ref[:, at], kbuf[:, at], vbuf[:, at], fix)

    per = cw // 128
    forward(0)
    own_copies[5].wait()
    for copy in own_copies[:2]:
        copy.wait()
    forward(1)
    forward(2)
    for c in range(CHUNKS):
        landed(c)
        pl.loop(c * per, (c + 1) * per, unroll=per)(local_pair)
        if c == 0:
            forward(3)
            spread(0, one)
        if c == 1:
            spread(0, two)
            relay(0, one)
            spread(1, one)
        if c == 2:
            spread(0, three)
            relay(0, two)
            spread(1, two)
            corner(0, one)
    relay(0, three)
    corner(0, two)
    corner(0, three)
    relay(1, one)
    own_copies[6].wait()
    own_copies[7].wait()
    gathered(0)

    projected = jnp.dot(lo[...], wo[...], preferred_element_type=jnp.float32)
    hidden = (tok_ref[...].astype(jnp.float32) + projected).astype(jnp.bfloat16)
    hid_ref[...] = hidden
    wide = hidden.astype(jnp.float32)
    inverse = lax.rsqrt(jnp.mean(wide * wide, axis=1, keepdims=True) + 1e-06)
    nbuf[pl.ds(0, tokens), :] = (wide * inverse * gain_ref[...]).astype(jnp.bfloat16)

    def block(s):
        return nbuf.at[pl.ds(s * tokens, tokens)]

    def ex_copy(s):
        return rc(block(0), block(s), ex_s.at[s], ex_r.at[s], line_dev(s))

    staged = n_lat == 4

    def direct(s, act):
        if staged and s == 3:
            pl.when(z != 0)(act)
        elif staged and s == 1:
            pl.when(z != n_lat - 1)(act)
        else:
            act()

    up_copy = rc(block(2), block(3), ex_s.at[0], ex_r.at[3], lat_dev(1))
    down_copy = rc(block(2), block(1), ex_s.at[0], ex_r.at[1], lat_dev(-1))

    for s in (2, 3, 1, 4):
        direct(s, lambda: ex_copy(s).start())
    spread(1, three)
    relay(1, two)
    corner(1, one)
    ex_copy(2).wait_recv()
    if staged:
        pl.when(z == 2)(lambda: up_copy.start())
        pl.when(z == 1)(lambda: down_copy.start())
    relay(1, three)
    corner(1, two)
    corner(1, three)
    gathered(1)

    tile = 512

    def project(at, count, column):
        left_rows = nbuf[pl.ds(at, count), :]
        weight = wg[:, pl.ds(pl.multiple_of(column, tile), tile)]
        return jnp.dot(left_rows, weight, preferred_element_type=jnp.float32).astype(jnp.bfloat16)

    def keys_values(at, count):
        @pl.loop(0, width // tile)
        def _(t):
            here = pl.ds(pl.multiple_of(t * tile, tile), tile)
            gk[pl.ds(at, count), here] = project(at, count, width + t * tile)
            gv[pl.ds(at, count), here] = project(at, count, 2 * width + t * tile)

    @pl.loop(0, width // tile)
    def _(t):
        here = pl.ds(pl.multiple_of(t * tile, tile), tile)
        gq[:, here] = project(0, tokens, t * tile)

    for s in (1, 3, 4):
        ex_copy(s).wait_recv()
    keys_values(0, (STEPS + 1) * tokens)

    def global_pair(h):
        at = pl.ds(pl.multiple_of(h * 128, 128), 128)

        def fix(s):
            edge = s.shape[1] - 128
            last = s[:, edge:]
            key = lax.broadcasted_iota(jnp.int32, last.shape, 1)
            last = jnp.where(key < (STEPS + 1) * tokens - edge, last, NEG)
            return jnp.concatenate([s[:, :edge], last], axis=1)

        att_ref[:, at] = two_heads(gq[:, at], gk[:, at], gv[:, at], fix)

    pl.loop(0, width // 128, unroll=4)(global_pair)

    for c in range(CHUNKS):
        for a in range(2):
            for way in range(2):
                lon_copy(a, 1, way, c).wait_send()

        @pl.when(has_up)
        def _():
            for a in range(2):
                lat_copy(a, 0, c).wait_send()
                for way in range(2):
                    lon_copy(a, 2, way, c).wait_send()

        @pl.when(has_down)
        def _():
            for a in range(2):
                lat_copy(a, 1, c).wait_send()
                for way in range(2):
                    lon_copy(a, 0, way, c).wait_send()

    for a in range(2):
        def sent(way, d):
            t = shard_of(way, d)
            wp_copy(a, t, j).wait_send()
            for e in range(dims):
                wx_copy(a, t, e, j).wait_send()
                if corners:
                    wh_copy(a, t, e, across(j, e)).wait_send()
            for e in range(dims + corners):
                wm_copy(a, t, e, across(j, e)).wait_send()

        each(range(1, n_lat), sent)
        for way, d in routes:
            pl.when(onward(way, d))(lambda: w1_copy(a, way, d).wait_send())
    for s in range(1, STEPS + 1):
        direct(s, lambda: ex_copy(s).wait_send())
    if staged:
        pl.when(z == 2)(lambda: up_copy.wait_send())
        pl.when(z == 1)(lambda: down_copy.wait_send())


def body(tokens, query_local, key_local, value_local, position_bias, output_weight, norm_gain, global_weight):
    n_lon = lax.axis_size("lon")
    n_lat = lax.axis_size("lat")
    lon_cells, lat_cells, width = tokens.shape
    count = lon_cells * lat_cells
    heads, window, _ = position_bias.shape
    rows = output_weight.shape[0]
    pieces = min(n_lon, 8 if rows >= 256 else 4)

    def flat(x):
        return x.reshape(count, width)

    lanes = -(-(6 * count) // 128) * 128
    keys = -(-((STEPS + 1) * count) // 128) * 128
    vmem = pl.BlockSpec(memory_space=pltpu.VMEM)
    hbm = pl.BlockSpec(memory_space=pltpu.HBM)
    dma = pltpu.SemaphoreType.DMA
    bf16 = jnp.bfloat16
    hidden, attended = pl.pallas_call(
        functools.partial(kernel, n_lon, n_lat, pieces),
        out_shape=(jax.ShapeDtypeStruct((count, width), bf16),) * 2,
        in_specs=[hbm] * 8,
        out_specs=(vmem, vmem),
        scratch_shapes=[
            pltpu.VMEM((count, width), bf16),
            pltpu.VMEM((count, width), bf16),
            pltpu.VMEM((window, heads, window), jnp.float32),
            pltpu.VMEM((heads, 384), jnp.float32),
            pltpu.VMEM((1, width), jnp.float32),
            pltpu.VMEM((lanes, width), bf16),
            pltpu.VMEM((lanes, width), bf16),
            pltpu.VMEM((width, width), bf16),
            pltpu.VMEM((width, 3 * width), bf16),
            pltpu.VMEM((heads * 8, lanes), jnp.float32),
            pltpu.VMEM((count, width), bf16),
            pltpu.VMEM(((STEPS + 1) * count, width), bf16),
            pltpu.VMEM((count, width), bf16),
            pltpu.VMEM((keys, width), bf16),
            pltpu.VMEM((keys, width), bf16),
            dma((8,)),
            dma((2, 2, CHUNKS)),
            dma((2, 2, CHUNKS)),
            dma((2, 3, 2, CHUNKS)),
            dma((2, 3, 2, CHUNKS)),
            dma((2, 2, n_lat)),
            dma((2, 2, n_lat)),
            dma((2, n_lat)),
            dma((2, n_lat)),
            dma((2, n_lat, 2)),
            dma((2, n_lat, 2)),
            dma((2, n_lat, 2)),
            dma((2, n_lat, 2)),
            dma((2, n_lat, 3)),
            dma((2, n_lat, 3)),
            dma((STEPS + 1,)),
            dma((STEPS + 1,)),
        ],
        compiler_params=pltpu.CompilerParams(
            collective_id=0, has_side_effects=True, vmem_limit_bytes=60 * 1024 * 1024
        ),
    )(
        flat(tokens),
        flat(query_local),
        flat(key_local),
        flat(value_local),
        jnp.transpose(position_bias, (1, 0, 2)),
        output_weight,
        norm_gain.reshape(1, width),
        global_weight,
    )
    return hidden.reshape(tokens.shape), attended.reshape(tokens.shape)


def solution(mesh):
    return jax.shard_map(
        body,
        mesh=mesh,
        in_specs=(
            P("lon", "lat", None),
            P("lon", "lat", None),
            P("lon", "lat", None),
            P("lon", "lat", None),
            P(),
            P("lat", None),
            P(),
            P("lat", None),
        ),
        out_specs=(P("lon", "lat", None), P("lon", "lat", None)),
        check_vma=False,
    )
```

```python
import functools

import jax
import jax.numpy as jnp
from jax import lax
from jax.experimental import pallas as pl
from jax.experimental.pallas import tpu as pltpu
from jax.sharding import PartitionSpec as P

STEPS = 4
CHUNKS = 4
NEG = -1e30
MESH = pl.DeviceIdType.MESH


def kernel(
    n_lon,
    n_lat,
    pieces,
    tok_hbm,
    q_hbm,
    k_hbm,
    v_hbm,
    b_hbm,
    wo_hbm,
    gain_hbm,
    wg_hbm,
    hid_ref,
    att_ref,
    tok_ref,
    q_ref,
    b_ref,
    tab,
    gain_ref,
    kbuf,
    vbuf,
    wo,
    wg,
    rbuf,
    lo,
    nbuf,
    gq,
    gk,
    gv,
    own_sem,
    lat_s,
    lat_r,
    lon_s,
    lon_r,
    w1_s,
    w1_r,
    wp_s,
    wp_r,
    wx_s,
    wx_r,
    wh_s,
    wh_r,
    wm_s,
    wm_r,
    ex_s,
    ex_r,
):
    i = lax.axis_index("lon")
    z = lax.axis_index("lat")
    rows = wo_hbm.shape[0]
    part = rows // pieces
    tokens, width = tok_ref.shape
    half = tokens // 2
    seg = 2 * tokens
    cw = width // CHUNKS
    j = lax.rem(i, pieces)
    base = i - j
    dims = pieces.bit_length() - 2

    def flip(at, bit):
        return at + bit - 2 * bit * lax.rem(at // bit, 2)

    mate = base + flip(j, 1)
    p = i * n_lat + z
    total = n_lon * n_lat

    def lat_dev(d):
        return (i, lax.rem(z + d + n_lat, n_lat))

    def lon_dev(d):
        return (lax.rem(i + d + n_lon, n_lon), z)

    def side(e):
        return (base + flip(j, 2 << e), z)

    def line_dev(s):
        t = lax.rem(p + s + total, total)
        return (t // n_lat, lax.rem(t, n_lat))

    def rc(src, dst, ssem, rsem, dev):
        return pltpu.make_async_remote_copy(
            src_ref=src, dst_ref=dst, send_sem=ssem, recv_sem=rsem, device_id=dev, device_id_type=MESH
        )

    barrier = pltpu.get_barrier_semaphore()
    greet = [lat_dev(1), lat_dev(-1)]
    greet += [lon_dev(1), lon_dev(-1), (mate, z)]
    greet += [side(e) for e in range(dims)]
    greet += [line_dev(-s) for s in range(1, STEPS + 1)]
    for dev in greet:
        pl.semaphore_signal(barrier, inc=1, device_id=dev, device_id_type=MESH)

    pairs = ((k_hbm, kbuf), (v_hbm, vbuf))
    weights = ((wo_hbm, wo), (wg_hbm, wg))
    own_copies = []
    for a, (src, dst) in enumerate(pairs):
        own_copies.append(
            pltpu.make_async_copy(src, dst.at[pl.ds(seg + half, tokens)], own_sem.at[a])
        )
    for a, (src, dst) in enumerate(weights):
        own_copies.append(
            pltpu.make_async_copy(
                src, dst.at[pl.ds(pl.multiple_of(z * rows, 16), rows)], own_sem.at[2 + a]
            )
        )
    singles = ((b_hbm, b_ref), (q_hbm, q_ref), (tok_hbm, tok_ref), (gain_hbm, gain_ref))
    for a, (src, dst) in enumerate(singles):
        own_copies.append(pltpu.make_async_copy(src, dst, own_sem.at[4 + a]))
    for at in (4, 0, 1, 5, 2, 3, 6, 7):
        own_copies[at].start()
    pl.semaphore_wait(barrier, len(greet))

    def cols(c):
        return pl.ds(c * cw, cw)

    def lat_copy(a, way, c):
        src, dst = pairs[a]
        at = 0 if way == 0 else 2
        return rc(
            src.at[:, cols(c)],
            dst.at[pl.ds(at * seg + half, tokens), cols(c)],
            lat_s.at[a, way, c],
            lat_r.at[a, way, c],
            lat_dev(1 if way == 0 else -1),
        )

    def lon_copy(a, s, way, c):
        src, dst = pairs[a]
        if s == 1:
            source = src.at[pl.ds(half if way == 0 else 0, half), cols(c)]
        else:
            source = dst.at[pl.ds(s * seg + (tokens if way == 0 else half), half), cols(c)]
        return rc(
            source,
            dst.at[pl.ds(s * seg + (0 if way == 0 else half + tokens), half), cols(c)],
            lon_s.at[a, s, way, c],
            lon_r.at[a, s, way, c],
            lon_dev(1 if way == 0 else -1),
        )

    has_up = z < n_lat - 1
    has_down = z > 0

    routes = [(way, d) for d in range(1, n_lat) for way in (1, -1)]

    def shard_of(way, d):
        return z - way * d

    def exists(way, d):
        return (shard_of(way, d) >= 0) & (shard_of(way, d) < n_lat)

    def w_rows(shard, piece):
        return pl.ds(pl.multiple_of(shard * rows + piece * part, 16), part)

    def w_move(a, shard, piece, ssem, rsem, dev):
        ref = weights[a][1].at[w_rows(shard, piece)]
        return rc(ref, ref, ssem, rsem, dev)

    def w1_copy(a, way, d):
        shard = shard_of(way, d - 1)
        sems = (w1_s.at[a, max(way, 0), d], w1_r.at[a, max(way, 0), d])
        if d > 1:
            return w_move(a, shard, j, *sems, lat_dev(way))
        src, dst = weights[a]
        piece = src.at[pl.ds(pl.multiple_of(j * part, 16), part)]
        return rc(piece, dst.at[w_rows(z, j)], *sems, lat_dev(way))

    def w1_wait(a, way, d):
        sems = (w1_s.at[a, max(way, 0), d], w1_r.at[a, max(way, 0), d])
        w_move(a, shard_of(way, d), j, *sems, lat_dev(way)).wait_recv()

    def onward(way, d):
        return exists(way, d - 1) & (has_up if way > 0 else has_down)

    def wp_copy(a, t, piece):
        return w_move(a, t, piece, wp_s.at[a, t], wp_r.at[a, t], (mate, z))

    def w_half(a, t, piece, e, ssem, rsem, dev):
        size = part // 2
        at = t * rows + piece * part + e * size
        ref = weights[a][1].at[pl.ds(pl.multiple_of(at, 16), size)]
        return rc(ref, ref, ssem, rsem, dev)

    def wx_copy(a, t, e, piece):
        return w_move(a, t, piece, wx_s.at[a, t, e], wx_r.at[a, t, e], side(e))

    def wh_copy(a, t, e, piece):
        return w_half(a, t, piece, e, wh_s.at[a, t, e], wh_r.at[a, t, e], side(1 - e))

    def wm_copy(a, t, e, piece):
        return w_move(a, t, piece, wm_s.at[a, t, e], wm_r.at[a, t, e], (mate, z))

    mate_piece = flip(j, 1)
    corners = 1 if dims == 2 else 0

    def across(at, e):
        return flip(at, 2 << e) if e < 2 else flip(flip(at, 2), 4)

    def each(ds, step):
        for way, d in routes:
            if d in ds:
                pl.when(exists(way, d))(functools.partial(step, way, d))

    def spread(a, ds):
        def step(way, d):
            w1_wait(a, way, d)
            if d + 1 < n_lat:
                pl.when(onward(way, d + 1))(lambda: w1_copy(a, way, d + 1).start())
            t = shard_of(way, d)
            for e in range(dims):
                wx_copy(a, t, e, j).start()
            wp_copy(a, t, j).start()

        each(ds, step)

    def relay(a, ds):
        def step(way, d):
            t = shard_of(way, d)
            for e in range(dims):
                piece = across(j, e)
                wx_copy(a, t, e, piece).wait_recv()
                if corners:
                    wh_copy(a, t, e, piece).start()
                wm_copy(a, t, e, piece).start()

        each(ds, step)

    def corner(a, ds):
        def step(way, d):
            t = shard_of(way, d)
            piece = across(j, 2)
            for e in range(2):
                wh_copy(a, t, e, piece).wait_recv()
            wm_copy(a, t, 2, piece).start()

        if corners:
            each(ds, step)

    def gathered(a):
        def step(way, d):
            t = shard_of(way, d)
            wp_copy(a, t, mate_piece).wait_recv()
            for e in range(dims + corners):
                wm_copy(a, t, e, across(mate_piece, e)).wait_recv()

        own_copies[2 + a].wait()
        each(range(1, n_lat), step)

    one, two, three = (1,), (2,), tuple(range(3, n_lat))

    for a in range(2):
        for way in (1, -1):
            pl.when(onward(way, 1))(lambda: w1_copy(a, way, 1).start())

    for c in range(CHUNKS):
        @pl.when(has_up)
        def _():
            for a in range(2):
                lat_copy(a, 0, c).start()

        @pl.when(has_down)
        def _():
            for a in range(2):
                lat_copy(a, 1, c).start()

        for a in range(2):
            for way in range(2):
                lon_copy(a, 1, way, c).start()

    pad_rows = kbuf.shape[0] - 3 * seg
    for ref in (kbuf, vbuf):
        ref[pl.ds(3 * seg, pad_rows), :] = jnp.zeros((pad_rows, width), jnp.bfloat16)

        @pl.when(jnp.logical_not(has_down))
        def _():
            ref[pl.ds(0, seg), :] = jnp.zeros((seg, width), jnp.bfloat16)

        @pl.when(jnp.logical_not(has_up))
        def _():
            ref[pl.ds(2 * seg, seg), :] = jnp.zeros((seg, width), jnp.bfloat16)

    for ref in (gk, gv):
        pad = ref.shape[0] - (STEPS + 1) * tokens
        ref[pl.ds((STEPS + 1) * tokens, pad), :] = jnp.zeros((pad, width), jnp.bfloat16)

    lanes = kbuf.shape[0]
    own_copies[4].wait()
    window = b_ref.shape[0]
    tab[...] = jnp.zeros_like(tab)
    for r in range(window):
        tab[:, r * 24 : r * 24 + window] = b_ref[r]
    heads = tab.shape[0]
    flat = jnp.concatenate(
        [jnp.broadcast_to(tab[h : h + 1, :], (8, tab.shape[1])) for h in range(heads)], axis=0
    )
    row_id = lax.broadcasted_iota(jnp.int32, flat.shape, 0)
    shifted = jnp.zeros_like(flat)
    for r in range(8):
        shifted = jnp.where(lax.rem(row_id, 8) == r, pltpu.roll(flat, r + 2, 1), shifted)
    lane = lax.broadcasted_iota(jnp.int32, (flat.shape[1], lanes), 1)
    spot = lax.broadcasted_iota(jnp.int32, (flat.shape[1], lanes), 0)
    at_seg = (lane >= seg).astype(jnp.int32) + (lane >= 2 * seg).astype(jnp.int32)
    inner = lane - at_seg * seg
    wanted = lax.shift_right_logical(inner, 3) * 24 + at_seg * 8 + (inner & 7)
    pick = jnp.where(spot == wanted, 1.0, 0.0).astype(jnp.bfloat16)
    first = shifted.astype(jnp.bfloat16)
    rest = shifted - first.astype(jnp.float32)
    second = rest.astype(jnp.bfloat16)
    third = (rest - second.astype(jnp.float32)).astype(jnp.bfloat16)
    bias = jnp.dot(first, pick, preferred_element_type=jnp.float32)
    bias = bias + jnp.dot(second, pick, preferred_element_type=jnp.float32)
    bias = bias + jnp.dot(third, pick, preferred_element_type=jnp.float32)
    lane = lax.broadcasted_iota(jnp.int32, bias.shape, 1)
    jrow = lax.rem(lax.broadcasted_iota(jnp.int32, bias.shape, 0), 8)
    at_seg = (lane >= seg).astype(jnp.int32) + (lane >= 2 * seg).astype(jnp.int32)
    inner = lane - at_seg * seg
    index = at_seg * 8 + (inner & 7) - jrow - 2
    low_lane = jnp.where(has_down, 0, seg)
    high_lane = jnp.where(has_up, 3 * seg, 2 * seg)
    fits = (inner < 13 * 8) & (index >= 0) & (index < 13) & (lane >= low_lane) & (lane < high_lane)
    rbuf[...] = jnp.where(fits, bias, NEG)

    def forward(c):
        @pl.when(has_down)
        def _():
            for a in range(2):
                lat_copy(a, 0, c).wait_recv()
                for way in range(2):
                    lon_copy(a, 0, way, c).start()

        @pl.when(has_up)
        def _():
            for a in range(2):
                lat_copy(a, 1, c).wait_recv()
                for way in range(2):
                    lon_copy(a, 2, way, c).start()

    def landed(c):
        for a in range(2):
            for way in range(2):
                lon_copy(a, 1, way, c).wait_recv()

        @pl.when(has_down)
        def _():
            for a in range(2):
                for way in range(2):
                    lon_copy(a, 0, way, c).wait_recv()

        @pl.when(has_up)
        def _():
            for a in range(2):
                for way in range(2):
                    lon_copy(a, 2, way, c).wait_recv()

    left = (lax.broadcasted_iota(jnp.int32, (tokens, 128), 1) < 64).astype(jnp.float32)
    left_mask = left.astype(jnp.bfloat16)
    right_mask = (1.0 - left).astype(jnp.bfloat16)

    def two_heads(q2, k2, v2, fix):
        q2 = q2 * jnp.bfloat16(0.125)
        qq = jnp.concatenate([q2 * left_mask, q2 * right_mask], axis=0)
        s = lax.dot_general(qq, k2, (((1,), (1,)), ((), ())), preferred_element_type=jnp.float32)
        s = fix(s)
        e = jnp.exp(s - jnp.max(s, axis=1, keepdims=True))
        t = jnp.sum(e, axis=1, keepdims=True)
        o = jnp.dot(e.astype(jnp.bfloat16), v2, preferred_element_type=jnp.float32) / t
        return jnp.where(left > 0.5, o[:tokens], o[tokens:]).astype(jnp.bfloat16)

    def local_pair(h):
        at = pl.ds(pl.multiple_of(h * 128, 128), 128)

        def fix(s):
            parts = []
            for head in range(2):
                r = rbuf[pl.ds(pl.multiple_of(h * 16 + head * 8, 8), 8), :]
                for col in range(tokens // 8):
                    parts.append(r if col == 0 else pltpu.roll(r, col * 8, 1))
            return s + jnp.concatenate(parts, axis=0)

        lo[:, at] = two_heads(q_ref[:, at], kbuf[:, at], vbuf[:, at], fix)

    per = cw // 128
    spread(0, one)
    spread(1, one)
    forward(0)
    forward(1)
    own_copies[5].wait()
    for copy in own_copies[:2]:
        copy.wait()
    for c in range(CHUNKS):
        landed(c)
        pl.loop(c * per, (c + 1) * per, unroll=per)(local_pair)
        if c == 0:
            forward(2)
            spread(0, two)
            spread(1, two)
            relay(0, one)
        if c == 1:
            forward(3)
            spread(0, three)
            spread(1, three)
            relay(1, one)
            relay(0, two)
        if c == 2:
            corner(0, one)
            relay(1, two)
            relay(0, three)
            corner(0, two)
            corner(1, one)
    corner(0, three)
    own_copies[6].wait()
    own_copies[7].wait()
    gathered(0)

    def halo_sent():
        for c in range(CHUNKS):
            for a in range(2):
                for way in range(2):
                    lon_copy(a, 1, way, c).wait_send()

            @pl.when(has_up)
            def _():
                for a in range(2):
                    lat_copy(a, 0, c).wait_send()
                    for way in range(2):
                        lon_copy(a, 2, way, c).wait_send()

            @pl.when(has_down)
            def _():
                for a in range(2):
                    lat_copy(a, 1, c).wait_send()
                    for way in range(2):
                        lon_copy(a, 0, way, c).wait_send()

    def weights_sent(a):
        def sent(way, d):
            t = shard_of(way, d)
            wp_copy(a, t, j).wait_send()
            for e in range(dims):
                wx_copy(a, t, e, j).wait_send()
                if corners:
                    wh_copy(a, t, e, across(j, e)).wait_send()
            for e in range(dims + corners):
                wm_copy(a, t, e, across(j, e)).wait_send()

        each(range(1, n_lat), sent)
        for way, d in routes:
            pl.when(onward(way, d))(lambda: w1_copy(a, way, d).wait_send())
    projected = jnp.dot(lo[...], wo[...], preferred_element_type=jnp.float32)
    hidden = (tok_ref[...].astype(jnp.float32) + projected).astype(jnp.bfloat16)
    hid_ref[...] = hidden
    wide = hidden.astype(jnp.float32)
    inverse = lax.rsqrt(jnp.mean(wide * wide, axis=1, keepdims=True) + 1e-06)
    nbuf[pl.ds(0, tokens), :] = (wide * inverse * gain_ref[...]).astype(jnp.bfloat16)

    def block(s):
        return nbuf.at[pl.ds(s * tokens, tokens)]

    def ex_copy(s):
        return rc(block(0), block(s), ex_s.at[s], ex_r.at[s], line_dev(s))

    staged = n_lat == 4

    def direct(s, act):
        if staged and s == 3:
            pl.when(z != 0)(act)
        elif staged and s == 1:
            pl.when(z != n_lat - 1)(act)
        else:
            act()

    up_copy = rc(block(2), block(3), ex_s.at[0], ex_r.at[3], lat_dev(1))
    down_copy = rc(block(2), block(1), ex_s.at[0], ex_r.at[1], lat_dev(-1))

    for s in (2, 3, 1, 4):
        direct(s, lambda: ex_copy(s).start())
    relay(1, three)
    corner(1, two)
    halo_sent()
    weights_sent(0)
    ex_copy(2).wait_recv()
    if staged:
        pl.when(z == 2)(lambda: up_copy.start())
        pl.when(z == 1)(lambda: down_copy.start())
    corner(1, three)
    gathered(1)

    tile = 512

    def project(at, count, column):
        left_rows = nbuf[pl.ds(at, count), :]
        weight = wg[:, pl.ds(pl.multiple_of(column, tile), tile)]
        return jnp.dot(left_rows, weight, preferred_element_type=jnp.float32).astype(jnp.bfloat16)

    def keys_values(at, count):
        @pl.loop(0, width // tile)
        def _(t):
            here = pl.ds(pl.multiple_of(t * tile, tile), tile)
            gk[pl.ds(at, count), here] = project(at, count, width + t * tile)
            gv[pl.ds(at, count), here] = project(at, count, 2 * width + t * tile)

    @pl.loop(0, width // tile)
    def _(t):
        here = pl.ds(pl.multiple_of(t * tile, tile), tile)
        gq[:, here] = project(0, tokens, t * tile)

    for s in (1, 3, 4):
        ex_copy(s).wait_recv()
    keys_values(0, (STEPS + 1) * tokens)

    def global_pair(h):
        at = pl.ds(pl.multiple_of(h * 128, 128), 128)

        def fix(s):
            edge = s.shape[1] - 128
            last = s[:, edge:]
            key = lax.broadcasted_iota(jnp.int32, last.shape, 1)
            last = jnp.where(key < (STEPS + 1) * tokens - edge, last, NEG)
            return jnp.concatenate([s[:, :edge], last], axis=1)

        att_ref[:, at] = two_heads(gq[:, at], gk[:, at], gv[:, at], fix)

    pl.loop(0, width // 128, unroll=4)(global_pair)

    weights_sent(1)
    for s in range(1, STEPS + 1):
        direct(s, lambda: ex_copy(s).wait_send())
    if staged:
        pl.when(z == 2)(lambda: up_copy.wait_send())
        pl.when(z == 1)(lambda: down_copy.wait_send())


def body(tokens, query_local, key_local, value_local, position_bias, output_weight, norm_gain, global_weight):
    n_lon = lax.axis_size("lon")
    n_lat = lax.axis_size("lat")
    lon_cells, lat_cells, width = tokens.shape
    count = lon_cells * lat_cells
    heads, window, _ = position_bias.shape
    rows = output_weight.shape[0]
    pieces = min(n_lon, 8 if rows >= 256 else 4)

    def flat(x):
        return x.reshape(count, width)

    lanes = -(-(6 * count) // 128) * 128
    keys = -(-((STEPS + 1) * count) // 128) * 128
    vmem = pl.BlockSpec(memory_space=pltpu.VMEM)
    hbm = pl.BlockSpec(memory_space=pltpu.HBM)
    dma = pltpu.SemaphoreType.DMA
    bf16 = jnp.bfloat16
    hidden, attended = pl.pallas_call(
        functools.partial(kernel, n_lon, n_lat, pieces),
        out_shape=(jax.ShapeDtypeStruct((count, width), bf16),) * 2,
        in_specs=[hbm] * 8,
        out_specs=(vmem, vmem),
        scratch_shapes=[
            pltpu.VMEM((count, width), bf16),
            pltpu.VMEM((count, width), bf16),
            pltpu.VMEM((window, heads, window), jnp.float32),
            pltpu.VMEM((heads, 384), jnp.float32),
            pltpu.VMEM((1, width), jnp.float32),
            pltpu.VMEM((lanes, width), bf16),
            pltpu.VMEM((lanes, width), bf16),
            pltpu.VMEM((width, width), bf16),
            pltpu.VMEM((width, 3 * width), bf16),
            pltpu.VMEM((heads * 8, lanes), jnp.float32),
            pltpu.VMEM((count, width), bf16),
            pltpu.VMEM(((STEPS + 1) * count, width), bf16),
            pltpu.VMEM((count, width), bf16),
            pltpu.VMEM((keys, width), bf16),
            pltpu.VMEM((keys, width), bf16),
            dma((8,)),
            dma((2, 2, CHUNKS)),
            dma((2, 2, CHUNKS)),
            dma((2, 3, 2, CHUNKS)),
            dma((2, 3, 2, CHUNKS)),
            dma((2, 2, n_lat)),
            dma((2, 2, n_lat)),
            dma((2, n_lat)),
            dma((2, n_lat)),
            dma((2, n_lat, 2)),
            dma((2, n_lat, 2)),
            dma((2, n_lat, 2)),
            dma((2, n_lat, 2)),
            dma((2, n_lat, 3)),
            dma((2, n_lat, 3)),
            dma((STEPS + 1,)),
            dma((STEPS + 1,)),
        ],
        compiler_params=pltpu.CompilerParams(
            collective_id=0, has_side_effects=True, vmem_limit_bytes=60 * 1024 * 1024
        ),
    )(
        flat(tokens),
        flat(query_local),
        flat(key_local),
        flat(value_local),
        jnp.transpose(position_bias, (1, 0, 2)),
        output_weight,
        norm_gain.reshape(1, width),
        global_weight,
    )
    return hidden.reshape(tokens.shape), attended.reshape(tokens.shape)


def solution(mesh):
    return jax.shard_map(
        body,
        mesh=mesh,
        in_specs=(
            P("lon", "lat", None),
            P("lon", "lat", None),
            P("lon", "lat", None),
            P("lon", "lat", None),
            P(),
            P("lat", None),
            P(),
            P("lat", None),
        ),
        out_specs=(P("lon", "lat", None), P("lon", "lat", None)),
        check_vma=False,
    )
```

```python
import functools

import jax
import jax.numpy as jnp
from jax import lax
from jax.experimental import pallas as pl
from jax.experimental.pallas import tpu as pltpu
from jax.sharding import PartitionSpec as P

STEPS = 4
CHUNKS = 4
NEG = -1e30
MESH = pl.DeviceIdType.MESH


def kernel(
    n_lon,
    n_lat,
    pieces,
    tok_hbm,
    q_hbm,
    k_hbm,
    v_hbm,
    b_hbm,
    wo_hbm,
    gain_hbm,
    wg_hbm,
    hid_ref,
    att_ref,
    tok_ref,
    q_ref,
    b_ref,
    tab,
    gain_ref,
    kbuf,
    vbuf,
    wo,
    wg,
    rbuf,
    lo,
    nbuf,
    gq,
    gk,
    gv,
    own_sem,
    lat_s,
    lat_r,
    lon_s,
    lon_r,
    w1_s,
    w1_r,
    wp_s,
    wp_r,
    wx_s,
    wx_r,
    wh_s,
    wh_r,
    wm_s,
    wm_r,
    ex_s,
    ex_r,
):
    i = lax.axis_index("lon")
    z = lax.axis_index("lat")
    rows = wo_hbm.shape[0]
    part = rows // pieces
    tokens, width = tok_ref.shape
    half = tokens // 2
    seg = 2 * tokens
    cw = width // CHUNKS
    j = lax.rem(i, pieces)
    base = i - j
    dims = pieces.bit_length() - 2

    def flip(at, bit):
        return at + bit - 2 * bit * lax.rem(at // bit, 2)

    mate = base + flip(j, 1)
    p = i * n_lat + z
    total = n_lon * n_lat

    def lat_dev(d):
        return (i, lax.rem(z + d + n_lat, n_lat))

    def lon_dev(d):
        return (lax.rem(i + d + n_lon, n_lon), z)

    def side(e):
        return (base + flip(j, 2 << e), z)

    def line_dev(s):
        t = lax.rem(p + s + total, total)
        return (t // n_lat, lax.rem(t, n_lat))

    def rc(src, dst, ssem, rsem, dev):
        return pltpu.make_async_remote_copy(
            src_ref=src, dst_ref=dst, send_sem=ssem, recv_sem=rsem, device_id=dev, device_id_type=MESH
        )

    barrier = pltpu.get_barrier_semaphore()
    greet = [lat_dev(1), lat_dev(-1)]
    greet += [lon_dev(1), lon_dev(-1), (mate, z)]
    greet += [side(e) for e in range(dims)]
    greet += [line_dev(-s) for s in range(1, STEPS + 1)]
    for dev in greet:
        pl.semaphore_signal(barrier, inc=1, device_id=dev, device_id_type=MESH)

    pairs = ((k_hbm, kbuf), (v_hbm, vbuf))
    weights = ((wo_hbm, wo), (wg_hbm, wg))
    own_copies = []
    for a, (src, dst) in enumerate(pairs):
        own_copies.append(
            pltpu.make_async_copy(src, dst.at[pl.ds(seg + half, tokens)], own_sem.at[a])
        )
    for a, (src, dst) in enumerate(weights):
        own_copies.append(
            pltpu.make_async_copy(
                src, dst.at[pl.ds(pl.multiple_of(z * rows, 16), rows)], own_sem.at[2 + a]
            )
        )
    singles = ((b_hbm, b_ref), (q_hbm, q_ref), (tok_hbm, tok_ref), (gain_hbm, gain_ref))
    for a, (src, dst) in enumerate(singles):
        own_copies.append(pltpu.make_async_copy(src, dst, own_sem.at[4 + a]))
    for at in (4, 0, 1, 5, 2, 3, 6, 7):
        own_copies[at].start()
    pl.semaphore_wait(barrier, len(greet))

    def cols(c):
        return pl.ds(c * cw, cw)

    def lat_copy(a, way, c):
        src, dst = pairs[a]
        at = 0 if way == 0 else 2
        return rc(
            src.at[:, cols(c)],
            dst.at[pl.ds(at * seg + half, tokens), cols(c)],
            lat_s.at[a, way, c],
            lat_r.at[a, way, c],
            lat_dev(1 if way == 0 else -1),
        )

    def lon_copy(a, s, way, c):
        src, dst = pairs[a]
        if s == 1:
            source = src.at[pl.ds(half if way == 0 else 0, half), cols(c)]
        else:
            source = dst.at[pl.ds(s * seg + (tokens if way == 0 else half), half), cols(c)]
        return rc(
            source,
            dst.at[pl.ds(s * seg + (0 if way == 0 else half + tokens), half), cols(c)],
            lon_s.at[a, s, way, c],
            lon_r.at[a, s, way, c],
            lon_dev(1 if way == 0 else -1),
        )

    has_up = z < n_lat - 1
    has_down = z > 0

    routes = [(way, d) for d in range(1, n_lat) for way in (1, -1)]

    def shard_of(way, d):
        return z - way * d

    def exists(way, d):
        return (shard_of(way, d) >= 0) & (shard_of(way, d) < n_lat)

    def w_rows(shard, piece):
        return pl.ds(pl.multiple_of(shard * rows + piece * part, 16), part)

    def w_move(a, shard, piece, ssem, rsem, dev):
        ref = weights[a][1].at[w_rows(shard, piece)]
        return rc(ref, ref, ssem, rsem, dev)

    def w1_copy(a, way, d):
        shard = shard_of(way, d - 1)
        sems = (w1_s.at[a, max(way, 0), d], w1_r.at[a, max(way, 0), d])
        if d > 1:
            return w_move(a, shard, j, *sems, lat_dev(way))
        src, dst = weights[a]
        piece = src.at[pl.ds(pl.multiple_of(j * part, 16), part)]
        return rc(piece, dst.at[w_rows(z, j)], *sems, lat_dev(way))

    def w1_wait(a, way, d):
        sems = (w1_s.at[a, max(way, 0), d], w1_r.at[a, max(way, 0), d])
        w_move(a, shard_of(way, d), j, *sems, lat_dev(way)).wait_recv()

    def onward(way, d):
        return exists(way, d - 1) & (has_up if way > 0 else has_down)

    def wp_copy(a, t, piece):
        return w_move(a, t, piece, wp_s.at[a, t], wp_r.at[a, t], (mate, z))

    def w_half(a, t, piece, e, ssem, rsem, dev):
        size = part // 2
        at = t * rows + piece * part + e * size
        ref = weights[a][1].at[pl.ds(pl.multiple_of(at, 16), size)]
        return rc(ref, ref, ssem, rsem, dev)

    def wx_copy(a, t, e, piece):
        return w_move(a, t, piece, wx_s.at[a, t, e], wx_r.at[a, t, e], side(e))

    def wh_copy(a, t, e, piece):
        return w_half(a, t, piece, e, wh_s.at[a, t, e], wh_r.at[a, t, e], side(1 - e))

    def wm_copy(a, t, e, piece):
        return w_move(a, t, piece, wm_s.at[a, t, e], wm_r.at[a, t, e], (mate, z))

    mate_piece = flip(j, 1)
    corners = 1 if dims == 2 else 0

    def across(at, e):
        return flip(at, 2 << e) if e < 2 else flip(flip(at, 2), 4)

    def each(ds, step):
        for way, d in routes:
            if d in ds:
                pl.when(exists(way, d))(functools.partial(step, way, d))

    def spread(a, ds):
        def step(way, d):
            w1_wait(a, way, d)
            if d + 1 < n_lat:
                pl.when(onward(way, d + 1))(lambda: w1_copy(a, way, d + 1).start())
            t = shard_of(way, d)
            for e in range(dims):
                wx_copy(a, t, e, j).start()
            wp_copy(a, t, j).start()

        each(ds, step)

    def relay(a, ds):
        def step(way, d):
            t = shard_of(way, d)
            for e in range(dims):
                piece = across(j, e)
                wx_copy(a, t, e, piece).wait_recv()
                if corners:
                    wh_copy(a, t, e, piece).start()
                wm_copy(a, t, e, piece).start()

        each(ds, step)

    def corner(a, ds):
        def step(way, d):
            t = shard_of(way, d)
            piece = across(j, 2)
            for e in range(2):
                wh_copy(a, t, e, piece).wait_recv()
            wm_copy(a, t, 2, piece).start()

        if corners:
            each(ds, step)

    def gathered(a):
        def step(way, d):
            t = shard_of(way, d)
            wp_copy(a, t, mate_piece).wait_recv()
            for e in range(dims + corners):
                wm_copy(a, t, e, across(mate_piece, e)).wait_recv()

        own_copies[2 + a].wait()
        each(range(1, n_lat), step)

    one, two, three = (1,), (2,), tuple(range(3, n_lat))

    for c in range(CHUNKS):
        @pl.when(has_up)
        def _():
            for a in range(2):
                lat_copy(a, 0, c).start()

        @pl.when(has_down)
        def _():
            for a in range(2):
                lat_copy(a, 1, c).start()

        for a in range(2):
            for way in range(2):
                lon_copy(a, 1, way, c).start()

    for a in range(2):
        for way in (1, -1):
            pl.when(onward(way, 1))(lambda: w1_copy(a, way, 1).start())

    pad_rows = kbuf.shape[0] - 3 * seg
    for ref in (kbuf, vbuf):
        ref[pl.ds(3 * seg, pad_rows), :] = jnp.zeros((pad_rows, width), jnp.bfloat16)

        @pl.when(jnp.logical_not(has_down))
        def _():
            ref[pl.ds(0, seg), :] = jnp.zeros((seg, width), jnp.bfloat16)

        @pl.when(jnp.logical_not(has_up))
        def _():
            ref[pl.ds(2 * seg, seg), :] = jnp.zeros((seg, width), jnp.bfloat16)

    for ref in (gk, gv):
        pad = ref.shape[0] - (STEPS + 1) * tokens
        ref[pl.ds((STEPS + 1) * tokens, pad), :] = jnp.zeros((pad, width), jnp.bfloat16)

    lanes = kbuf.shape[0]
    own_copies[4].wait()
    window = b_ref.shape[0]
    tab[...] = jnp.zeros_like(tab)
    for r in range(window):
        tab[:, r * 24 : r * 24 + window] = b_ref[r]
    heads = tab.shape[0]
    flat = jnp.concatenate(
        [jnp.broadcast_to(tab[h : h + 1, :], (8, tab.shape[1])) for h in range(heads)], axis=0
    )
    row_id = lax.broadcasted_iota(jnp.int32, flat.shape, 0)
    shifted = jnp.zeros_like(flat)
    for r in range(8):
        shifted = jnp.where(lax.rem(row_id, 8) == r, pltpu.roll(flat, r + 2, 1), shifted)
    lane = lax.broadcasted_iota(jnp.int32, (flat.shape[1], lanes), 1)
    spot = lax.broadcasted_iota(jnp.int32, (flat.shape[1], lanes), 0)
    at_seg = (lane >= seg).astype(jnp.int32) + (lane >= 2 * seg).astype(jnp.int32)
    inner = lane - at_seg * seg
    wanted = lax.shift_right_logical(inner, 3) * 24 + at_seg * 8 + (inner & 7)
    pick = jnp.where(spot == wanted, 1.0, 0.0).astype(jnp.bfloat16)
    first = shifted.astype(jnp.bfloat16)
    rest = shifted - first.astype(jnp.float32)
    second = rest.astype(jnp.bfloat16)
    third = (rest - second.astype(jnp.float32)).astype(jnp.bfloat16)
    bias = jnp.dot(first, pick, preferred_element_type=jnp.float32)
    bias = bias + jnp.dot(second, pick, preferred_element_type=jnp.float32)
    bias = bias + jnp.dot(third, pick, preferred_element_type=jnp.float32)
    lane = lax.broadcasted_iota(jnp.int32, bias.shape, 1)
    jrow = lax.rem(lax.broadcasted_iota(jnp.int32, bias.shape, 0), 8)
    at_seg = (lane >= seg).astype(jnp.int32) + (lane >= 2 * seg).astype(jnp.int32)
    inner = lane - at_seg * seg
    index = at_seg * 8 + (inner & 7) - jrow - 2
    low_lane = jnp.where(has_down, 0, seg)
    high_lane = jnp.where(has_up, 3 * seg, 2 * seg)
    fits = (inner < 13 * 8) & (index >= 0) & (index < 13) & (lane >= low_lane) & (lane < high_lane)
    rbuf[...] = jnp.where(fits, bias, NEG)

    def forward(c):
        @pl.when(has_down)
        def _():
            for a in range(2):
                lat_copy(a, 0, c).wait_recv()
                for way in range(2):
                    lon_copy(a, 0, way, c).start()

        @pl.when(has_up)
        def _():
            for a in range(2):
                lat_copy(a, 1, c).wait_recv()
                for way in range(2):
                    lon_copy(a, 2, way, c).start()

    def landed(c):
        for a in range(2):
            for way in range(2):
                lon_copy(a, 1, way, c).wait_recv()

        @pl.when(has_down)
        def _():
            for a in range(2):
                for way in range(2):
                    lon_copy(a, 0, way, c).wait_recv()

        @pl.when(has_up)
        def _():
            for a in range(2):
                for way in range(2):
                    lon_copy(a, 2, way, c).wait_recv()

    left = (lax.broadcasted_iota(jnp.int32, (tokens, 128), 1) < 64).astype(jnp.float32)
    left_mask = left.astype(jnp.bfloat16)
    right_mask = (1.0 - left).astype(jnp.bfloat16)

    def two_heads(q2, k2, v2, fix):
        q2 = q2 * jnp.bfloat16(0.125)
        qq = jnp.concatenate([q2 * left_mask, q2 * right_mask], axis=0)
        s = lax.dot_general(qq, k2, (((1,), (1,)), ((), ())), preferred_element_type=jnp.float32)
        s = fix(s)
        e = jnp.exp(s - jnp.max(s, axis=1, keepdims=True))
        t = jnp.sum(e, axis=1, keepdims=True)
        o = jnp.dot(e.astype(jnp.bfloat16), v2, preferred_element_type=jnp.float32) / t
        return jnp.where(left > 0.5, o[:tokens], o[tokens:]).astype(jnp.bfloat16)

    def local_pair(h):
        at = pl.ds(pl.multiple_of(h * 128, 128), 128)

        def fix(s):
            parts = []
            for head in range(2):
                r = rbuf[pl.ds(pl.multiple_of(h * 16 + head * 8, 8), 8), :]
                for col in range(tokens // 8):
                    parts.append(r if col == 0 else pltpu.roll(r, col * 8, 1))
            return s + jnp.concatenate(parts, axis=0)

        lo[:, at] = two_heads(q_ref[:, at], kbuf[:, at], vbuf[:, at], fix)

    per = cw // 128
    forward(0)
    own_copies[5].wait()
    for copy in own_copies[:2]:
        copy.wait()
    forward(1)
    forward(2)
    for c in range(CHUNKS):
        landed(c)
        pl.loop(c * per, (c + 1) * per, unroll=per)(local_pair)
        if c == 0:
            forward(3)
            spread(0, one)
        if c == 1:
            spread(0, two)
            relay(0, one)
            spread(1, one)
        if c == 2:
            spread(0, three)
            relay(0, two)
            spread(1, two)
            corner(0, one)
    relay(0, three)
    corner(0, two)
    corner(0, three)
    relay(1, one)
    own_copies[6].wait()
    own_copies[7].wait()
    gathered(0)

    def halo_sent():
        for c in range(CHUNKS):
            for a in range(2):
                for way in range(2):
                    lon_copy(a, 1, way, c).wait_send()

            @pl.when(has_up)
            def _():
                for a in range(2):
                    lat_copy(a, 0, c).wait_send()
                    for way in range(2):
                        lon_copy(a, 2, way, c).wait_send()

            @pl.when(has_down)
            def _():
                for a in range(2):
                    lat_copy(a, 1, c).wait_send()
                    for way in range(2):
                        lon_copy(a, 0, way, c).wait_send()

    def weights_sent(a):
        def sent(way, d):
            t = shard_of(way, d)
            wp_copy(a, t, j).wait_send()
            for e in range(dims):
                wx_copy(a, t, e, j).wait_send()
                if corners:
                    wh_copy(a, t, e, across(j, e)).wait_send()
            for e in range(dims + corners):
                wm_copy(a, t, e, across(j, e)).wait_send()

        each(range(1, n_lat), sent)
        for way, d in routes:
            pl.when(onward(way, d))(lambda: w1_copy(a, way, d).wait_send())

    projected = jnp.dot(lo[...], wo[...], preferred_element_type=jnp.float32)
    hidden = (tok_ref[...].astype(jnp.float32) + projected).astype(jnp.bfloat16)
    hid_ref[...] = hidden
    wide = hidden.astype(jnp.float32)
    inverse = lax.rsqrt(jnp.mean(wide * wide, axis=1, keepdims=True) + 1e-06)
    nbuf[pl.ds(0, tokens), :] = (wide * inverse * gain_ref[...]).astype(jnp.bfloat16)

    def block(s):
        return nbuf.at[pl.ds(s * tokens, tokens)]

    def ex_copy(s):
        return rc(block(0), block(s), ex_s.at[s], ex_r.at[s], line_dev(s))

    staged = n_lat == 4

    def direct(s, act):
        if staged and s == 3:
            pl.when(z != 0)(act)
        elif staged and s == 1:
            pl.when(z != n_lat - 1)(act)
        else:
            act()

    up_copy = rc(block(2), block(3), ex_s.at[0], ex_r.at[3], lat_dev(1))
    down_copy = rc(block(2), block(1), ex_s.at[0], ex_r.at[1], lat_dev(-1))

    for s in (2, 3, 1, 4):
        direct(s, lambda: ex_copy(s).start())
    spread(1, three)
    relay(1, two)
    corner(1, one)
    ex_copy(2).wait_recv()
    if staged:
        pl.when(z == 2)(lambda: up_copy.start())
        pl.when(z == 1)(lambda: down_copy.start())
    relay(1, three)
    corner(1, two)
    halo_sent()
    weights_sent(0)
    corner(1, three)
    gathered(1)

    tile = 512

    def project(at, count, column):
        left_rows = nbuf[pl.ds(at, count), :]
        weight = wg[:, pl.ds(pl.multiple_of(column, tile), tile)]
        return jnp.dot(left_rows, weight, preferred_element_type=jnp.float32).astype(jnp.bfloat16)

    def keys_values(at, count):
        @pl.loop(0, width // tile)
        def _(t):
            here = pl.ds(pl.multiple_of(t * tile, tile), tile)
            gk[pl.ds(at, count), here] = project(at, count, width + t * tile)
            gv[pl.ds(at, count), here] = project(at, count, 2 * width + t * tile)

    @pl.loop(0, width // tile)
    def _(t):
        here = pl.ds(pl.multiple_of(t * tile, tile), tile)
        gq[:, here] = project(0, tokens, t * tile)

    keys_values(0, tokens)
    for s in (1, 3, 4):
        ex_copy(s).wait_recv()
    keys_values(tokens, STEPS * tokens)

    def global_pair(h):
        at = pl.ds(pl.multiple_of(h * 128, 128), 128)

        def fix(s):
            edge = s.shape[1] - 128
            last = s[:, edge:]
            key = lax.broadcasted_iota(jnp.int32, last.shape, 1)
            last = jnp.where(key < (STEPS + 1) * tokens - edge, last, NEG)
            return jnp.concatenate([s[:, :edge], last], axis=1)

        att_ref[:, at] = two_heads(gq[:, at], gk[:, at], gv[:, at], fix)

    pl.loop(0, width // 128, unroll=4)(global_pair)

    weights_sent(1)
    for s in range(1, STEPS + 1):
        direct(s, lambda: ex_copy(s).wait_send())
    if staged:
        pl.when(z == 2)(lambda: up_copy.wait_send())
        pl.when(z == 1)(lambda: down_copy.wait_send())


def body(tokens, query_local, key_local, value_local, position_bias, output_weight, norm_gain, global_weight):
    n_lon = lax.axis_size("lon")
    n_lat = lax.axis_size("lat")
    lon_cells, lat_cells, width = tokens.shape
    count = lon_cells * lat_cells
    heads, window, _ = position_bias.shape
    rows = output_weight.shape[0]
    pieces = min(n_lon, 8 if rows >= 256 else 4)

    def flat(x):
        return x.reshape(count, width)

    lanes = -(-(6 * count) // 128) * 128
    keys = -(-((STEPS + 1) * count) // 128) * 128
    vmem = pl.BlockSpec(memory_space=pltpu.VMEM)
    hbm = pl.BlockSpec(memory_space=pltpu.HBM)
    dma = pltpu.SemaphoreType.DMA
    bf16 = jnp.bfloat16
    hidden, attended = pl.pallas_call(
        functools.partial(kernel, n_lon, n_lat, pieces),
        out_shape=(jax.ShapeDtypeStruct((count, width), bf16),) * 2,
        in_specs=[hbm] * 8,
        out_specs=(vmem, vmem),
        scratch_shapes=[
            pltpu.VMEM((count, width), bf16),
            pltpu.VMEM((count, width), bf16),
            pltpu.VMEM((window, heads, window), jnp.float32),
            pltpu.VMEM((heads, 384), jnp.float32),
            pltpu.VMEM((1, width), jnp.float32),
            pltpu.VMEM((lanes, width), bf16),
            pltpu.VMEM((lanes, width), bf16),
            pltpu.VMEM((width, width), bf16),
            pltpu.VMEM((width, 3 * width), bf16),
            pltpu.VMEM((heads * 8, lanes), jnp.float32),
            pltpu.VMEM((count, width), bf16),
            pltpu.VMEM(((STEPS + 1) * count, width), bf16),
            pltpu.VMEM((count, width), bf16),
            pltpu.VMEM((keys, width), bf16),
            pltpu.VMEM((keys, width), bf16),
            dma((8,)),
            dma((2, 2, CHUNKS)),
            dma((2, 2, CHUNKS)),
            dma((2, 3, 2, CHUNKS)),
            dma((2, 3, 2, CHUNKS)),
            dma((2, 2, n_lat)),
            dma((2, 2, n_lat)),
            dma((2, n_lat)),
            dma((2, n_lat)),
            dma((2, n_lat, 2)),
            dma((2, n_lat, 2)),
            dma((2, n_lat, 2)),
            dma((2, n_lat, 2)),
            dma((2, n_lat, 3)),
            dma((2, n_lat, 3)),
            dma((STEPS + 1,)),
            dma((STEPS + 1,)),
        ],
        compiler_params=pltpu.CompilerParams(
            collective_id=0, has_side_effects=True, vmem_limit_bytes=60 * 1024 * 1024
        ),
    )(
        flat(tokens),
        flat(query_local),
        flat(key_local),
        flat(value_local),
        jnp.transpose(position_bias, (1, 0, 2)),
        output_weight,
        norm_gain.reshape(1, width),
        global_weight,
    )
    return hidden.reshape(tokens.shape), attended.reshape(tokens.shape)


def solution(mesh):
    return jax.shard_map(
        body,
        mesh=mesh,
        in_specs=(
            P("lon", "lat", None),
            P("lon", "lat", None),
            P("lon", "lat", None),
            P("lon", "lat", None),
            P(),
            P("lat", None),
            P(),
            P("lat", None),
        ),
        out_specs=(P("lon", "lat", None), P("lon", "lat", None)),
        check_vma=False,
    )
```
